32 devices in a mesh: dp: 2 (over core), ctx: 4 (over z), grp: 4 (over y, x).
Axes of the slice: x: 2, y: 2, z: 4, core: 2. Of those that a mesh axis runs over, the one named last changes fastest.
Arguments:
- projected: bfloat16 [4, 1024, 3, 4096], P('dp', 'ctx', None, 'grp'), may hold values from -6 to 6
- short_w: float32 [3, 3, 4096], P(None, None, 'grp'), may hold values from -2.5 to 2.5
- medium_h: bfloat16 [256, 128], P('grp'), may hold values from -3 to 3
- out_w: bfloat16 [4096, 4096], P('ctx', 'grp'), may hold values from -0.09375 to 0.09375
- grad_out: bfloat16 [4, 1024, 4096], P('dp', 'ctx', 'grp'), may hold values from -6 to 6
Outputs:
- block_out: bfloat16 [4, 1024, 4096], P('dp', 'ctx', 'grp')
- grad_projected: bfloat16 [4, 1024, 3, 4096], P('dp', 'ctx', None, 'grp')
- filter_grad: float32 [256, 128], P('grp')
- short_grad: float32 [3, 3, 4096], P(None, None, 'grp')
The draws below stay inside these ranges and needn't reach their ends.
All inputs are finite; a program needn't handle non-finite values.
Results may differ from the reference program's by a relative error of at most 0.0064.
Values may be sent and summed in bfloat16 or wider, within the bound.
No kernel may reach another device: no remote copies, remote signals or barrier semaphores. Data moves between devices by JAX's collectives and lax.ppermute only.
A program may use at most 128 MiB of HBM per device.

```python
import math
import jax
import jax.numpy as jnp
from jax import lax

D = 4096
G = 256
TAPS = 128
SHORT = 3
LEN = 1024
SEQS = 4


def draw_medium_h(key, part):
    noise_key, rate_key = jax.random.split(key)
    noise = jnp.clip(jax.random.normal(noise_key, (G, TAPS), jnp.float32), -4.0, 4.0)
    spans = jnp.exp(jax.random.uniform(rate_key, (G, 1), jnp.float32, math.log(4.0), math.log(512.0)))
    positions = jnp.arange(TAPS, dtype=jnp.float32)[None, :]
    values = noise * jnp.exp(-positions / spans) * jnp.sqrt(2.0 / spans + 1.0 / TAPS)
    return values.astype(jnp.bfloat16)


def level_of(key, shape, cuts, low, largest):
    factor_of, own = 1.0, jax.random.fold_in(key, 6)
    for axis_at, blocks in cuts:
        steps = jnp.exp(jax.random.uniform(jax.random.fold_in(own, axis_at), (blocks,), jnp.float32, low / len(cuts), largest / len(cuts)))
        factor_of = factor_of * jnp.repeat(steps, shape[axis_at] // blocks).reshape([-1 if axis == axis_at else 1 for axis in range(len(shape))])
    return factor_of


def normal_values(rng, shape, deviation, limit, pieces=(), kind=jnp.bfloat16):
    entries = jax.random.normal(rng, shape, jnp.float32) * deviation
    if len(pieces) > 0:
        entries = level_of(rng, shape, pieces, -0.22, 0.18) * entries
    return jnp.clip(entries, min=-limit, max=limit).astype(kind)


def setup_inputs(seed: int = 0) -> dict:
    splits = jax.random.split(jax.random.key(seed), 6)
    return {
        "projected": normal_values(splits[0], (SEQS, LEN, 3, D), 1.0, 6.0, ((0, 2), (1, 4), (3, 4))),
        "short_w": normal_values(splits[1], (3, SHORT, D), 0.4, 2.5, ((2, 4),), jnp.float32),
        "medium_h": draw_medium_h(jax.random.fold_in(splits[5], 71), 0),
        "out_w": normal_values(splits[3], (D, D), D ** -0.5, 0.09375, ((0, 4), (1, 4))),
        "grad_out": normal_values(splits[4], (SEQS, LEN, D), 1.0, 6.0, ((0, 2), (1, 4), (2, 4))),
    }


def windows(padded, block_rows, reach):
    seqs_here = padded.shape[0]
    block_count = (padded.shape[1] - reach) // block_rows
    extended = jnp.pad(padded, ((0, 0), (0, block_rows - reach), (0, 0), (0, 0)))
    leading = extended[:, :block_count * block_rows].reshape(seqs_here, block_count, block_rows, padded.shape[2], padded.shape[3])
    second = extended[:, block_rows:].reshape(seqs_here, block_count, block_rows, padded.shape[2], padded.shape[3])[:, :, :reach]
    return jnp.concatenate([leading, second], axis=2)

def banded(filters, block_rows):
    groups_here = filters.shape[0]
    tap_count = filters.shape[1]
    line_width = block_rows + tap_count
    padded_line = jnp.concatenate([filters, jnp.zeros((groups_here, block_rows), filters.dtype)], axis=1)
    tiled = jnp.broadcast_to(padded_line[:, None, :], (groups_here, block_rows, line_width)).reshape(groups_here, block_rows * line_width)
    return tiled[:, :block_rows * (line_width - 1)].reshape(groups_here, block_rows, line_width - 1)

def band_conv(padded, matrix, block_rows):
    reach = matrix.shape[2] - block_rows
    windowed = windows(padded, block_rows, reach)
    result = jnp.einsum('gtj,sbjgc->sbtgc', matrix.astype(jnp.float32), windowed.astype(jnp.float32))
    return result.reshape(padded.shape[0], padded.shape[1] - reach, padded.shape[2] * padded.shape[3])

def lag_sums(grad_blocks, windowed, tap_count):
    products = jnp.einsum('sbtgc,sbjgc->gtj', grad_blocks.astype(jnp.float32), windowed.astype(jnp.float32))
    groups_here = products.shape[0]
    block_rows = products.shape[1]
    line_width = products.shape[2]
    flat_rows = jnp.pad(products.reshape(groups_here, block_rows * line_width), ((0, 0), (0, block_rows)))
    skewed = flat_rows.reshape(groups_here, block_rows, line_width + 1)[:, :, :tap_count]
    return lax.optimization_barrier(jnp.sum(skewed, axis=1))[:, ::-1]

def featurize(padded, weights):
    short_reach = weights.shape[1] - 1
    axis_rows = padded.ndim - 3
    row_count = padded.shape[axis_rows] - short_reach
    total = None
    for offset in range(weights.shape[1]):
        start = short_reach - offset
        term = weights[:, offset, :] * lax.slice_in_dim(padded, start, start + row_count, axis=axis_rows)
        total = term if total is None else total + term
    return total

def adjoint(padded, weights):
    short_reach = weights.shape[1] - 1
    axis_rows = padded.ndim - 3
    row_count = padded.shape[axis_rows] - short_reach
    total = None
    for offset in range(weights.shape[1]):
        term = weights[:, offset, :] * lax.slice_in_dim(padded, offset, offset + row_count, axis=axis_rows)
        total = term if total is None else total + term
    return total

def short_sums(feature_grad, padded, short_taps):
    axis_rows = padded.ndim - 3
    row_count = feature_grad.shape[axis_rows]
    short_reach = short_taps - 1
    axes_summed = tuple(range(feature_grad.ndim - 2))
    terms = []
    for offset in range(short_taps):
        start = short_reach - offset
        shifted = lax.slice_in_dim(padded, start, start + row_count, axis=axis_rows)
        terms.append(lax.optimization_barrier(jnp.sum(feature_grad * shifted, axis=axes_summed)))
    return jnp.stack(terms, axis=1)

def reference(projected, short_w, medium_h, out_w, grad_out):
    tap_count = medium_h.shape[1]
    reach = tap_count - 1
    short_taps = short_w.shape[1]
    short_reach = short_taps - 1
    groups = medium_h.shape[0]
    group_size = D // groups
    block_rows = math.gcd(LEN, 128)
    causal = banded(medium_h[:, ::-1], block_rows)
    anticausal = banded(medium_h, block_rows)

    def one_sequence(carry, inputs):
        sequence, cotangent = inputs
        padded_input = jnp.pad(sequence.astype(jnp.float32), ((short_reach, 0), (0, 0), (0, 0)))
        features = featurize(padded_input, short_w)
        query = features[:, 0]
        keys = features[:, 1]
        values = features[:, 2]
        product = (keys * values).astype(jnp.bfloat16)
        product_pad = jnp.pad(product, ((reach, 0), (0, 0))).reshape(1, LEN + reach, groups, group_size)
        mixed = band_conv(product_pad, causal, block_rows)[0]
        gated = (query * mixed).astype(jnp.bfloat16)
        block_out = jnp.dot(gated, out_w, preferred_element_type=jnp.float32).astype(jnp.bfloat16)
        gated_grad = lax.optimization_barrier(jnp.dot(cotangent, out_w.T, preferred_element_type=jnp.float32).astype(jnp.bfloat16)).astype(jnp.float32)
        query_grad = gated_grad * mixed
        mix_grad = (gated_grad * query).astype(jnp.bfloat16)
        mix_pad = jnp.pad(mix_grad, ((0, reach), (0, 0))).reshape(1, LEN + reach, groups, group_size)
        product_grad = band_conv(mix_pad, anticausal, block_rows)[0]
        filter_part = lag_sums(mix_grad.reshape(1, LEN // block_rows, block_rows, groups, group_size), windows(product_pad, block_rows, reach), tap_count)
        feature_grad = jnp.stack([query_grad, product_grad * values, product_grad * keys], axis=1).astype(jnp.bfloat16)
        feature_float = feature_grad.astype(jnp.float32)
        grad_pad = jnp.pad(feature_float, ((0, short_reach), (0, 0), (0, 0)))
        input_grad = adjoint(grad_pad, short_w).astype(jnp.bfloat16)
        short_part = short_sums(feature_float, padded_input, short_taps)
        return ((carry[0] + filter_part, carry[1] + short_part), (block_out, input_grad))
    start_sums = (jnp.zeros((groups, tap_count), jnp.float32), jnp.zeros((3, short_taps, D), jnp.float32))
    sums, stacked = lax.scan(one_sequence, start_sums, (projected, grad_out))
    filter_grad = sums[0] / math.sqrt(SEQS * LEN * group_size)
    short_grad = sums[1] / math.sqrt(SEQS * LEN)
    return (stacked[0], stacked[1], filter_grad, short_grad)
```

```python
import functools
import math

import jax
import jax.numpy as jnp
from jax import lax
from jax.experimental import pallas as pl
from jax.experimental.pallas import tpu as pltpu
from jax.sharding import PartitionSpec as P

LANES = 128
HALO = 144
EXTRA = 16
F32 = jnp.float32
BF16 = jnp.bfloat16


def params(mib=32):
    return pltpu.CompilerParams(vmem_limit_bytes=mib * 1024 * 1024)


def shift(block, axis, distance, first=0):
    count = lax.axis_size(axis)
    if distance > 0:
        route = [(i, i + distance) for i in range(first, count - distance)]
    else:
        route = [(i, i + distance) for i in range(-distance, count - first)]
    return lax.ppermute(block, axis, route)


def pick_groups(stacked, rows, group_size):
    width = stacked.shape[1]
    lane = lax.broadcasted_iota(jnp.int32, (1, width), 1) % LANES
    groups = LANES // group_size
    total = stacked[:rows]
    for g in range(1, groups):
        total = jnp.where(lane >= g * group_size, stacked[g * rows : (g + 1) * rows], total)
    return total


def fill_band(line_ref, band_ref, rows):
    for g in range(line_ref.shape[0]):
        wide = jnp.broadcast_to(line_ref[g : g + 1, :], (rows, line_ref.shape[1]))
        moved = pltpu.roll(wide, 0, 1, stride=1, stride_axis=0)
        band_ref[g * rows : (g + 1) * rows, :] = moved.astype(BF16)


def features_kernel(x_ref, front_ref, w_ref, product_ref, q_ref, k_ref, v_ref, pad):
    seqs, rows = x_ref.shape[1], x_ref.shape[2]
    for s in range(seqs):
        found = []
        for j, out_ref in enumerate((q_ref, k_ref, v_ref)):
            own = s * 3 + j
            pad[own, 0:8] = front_ref[j, s]
            pad[own, 8 : 8 + rows] = x_ref[j, s].astype(F32)
            total = w_ref[j, 0:1] * pad[own, 8 : 8 + rows]
            total = total + w_ref[j, 1:2] * pad[own, 7 : 7 + rows]
            total = total + w_ref[j, 2:3] * pad[own, 6 : 6 + rows]
            out_ref[s] = total
            found.append(total)
        product_ref[s] = (found[1] * found[2]).astype(BF16)


def features(x, front, short_w):
    _, seqs, rows, width = x.shape
    at4 = lambda i: (0, 0, 0, i)
    at3 = lambda i: (0, 0, i)
    wide = pl.BlockSpec((seqs, rows, LANES), at3)
    shape = (seqs, rows, width)
    return pl.pallas_call(
        features_kernel,
        grid=(width // LANES,),
        in_specs=[
            pl.BlockSpec((3, seqs, rows, LANES), at4),
            pl.BlockSpec((3, seqs, 8, LANES), at4),
            pl.BlockSpec((3, 3, LANES), at3),
        ],
        out_specs=[wide] * 4,
        out_shape=[jax.ShapeDtypeStruct(shape, BF16)] + [jax.ShapeDtypeStruct(shape, F32)] * 3,
        scratch_shapes=[pltpu.VMEM((3 * seqs, rows + 8, LANES), F32)],
        compiler_params=params(),
        name="features",
    )(x, front, short_w)


def mix_kernel(group_size, line_ref, low_ref, high_ref, q_ref, mixed_ref, gated_ref, band, columns):
    seqs, rows = low_ref.shape[0], low_ref.shape[1]
    fill_band(line_ref, band, rows)
    for s in range(seqs):
        at = slice(s * LANES, (s + 1) * LANES)
        columns[:rows, at] = low_ref[s]
        columns[rows:, at] = high_ref[s]
    stacked = jnp.dot(band[...], columns[...], preferred_element_type=F32)
    mixed = pick_groups(stacked, rows, group_size)
    for s in range(seqs):
        part = mixed[:, s * LANES : (s + 1) * LANES]
        mixed_ref[s] = part
        gated_ref[s] = (q_ref[s] * part).astype(BF16)


def mix(line, low, low_at, high, high_at, query, query_at, rows, group_size):
    seqs, _, width = query.shape
    groups = LANES // group_size
    part = lambda at: pl.BlockSpec((seqs, rows, LANES), lambda i: (0, at, i))
    shape = (seqs, rows, width)
    return pl.pallas_call(
        functools.partial(mix_kernel, group_size),
        grid=(width // LANES,),
        in_specs=[
            pl.BlockSpec((groups, 2 * rows), lambda i: (i, 0)),
            part(low_at),
            part(high_at),
            part(query_at),
        ],
        out_specs=[part(0), part(0)],
        out_shape=[jax.ShapeDtypeStruct(shape, F32), jax.ShapeDtypeStruct(shape, BF16)],
        scratch_shapes=[
            pltpu.VMEM((groups * rows, 2 * rows), BF16),
            pltpu.VMEM((2 * rows, seqs * LANES), BF16),
        ],
        compiler_params=params(),
        name="mix",
    )(line, low, high, query)


def fetch_rows(pos_ref, own_ref, near, far, buffer, sems, slot, owner, at, half):
    here, core = pos_ref[0], pos_ref[1]
    steps = len(near) + 1
    step = lax.rem(here - owner + steps, steps)

    def copies(first, second, start):
        mine = pl.multiple_of(at + core * half, half)
        other = pl.multiple_of(at + (1 - core) * half, half)
        for which, (source, place) in enumerate(((first, mine), (second, other))):
            copy = pltpu.make_async_copy(
                source, buffer.at[slot, pl.ds(place, half)], sems.at[slot, which]
            )
            copy.start() if start else copy.wait()

    def begin():
        @pl.when(step == 0)
        def _():
            mine = pl.multiple_of(at + core * half, half)
            other = pl.multiple_of(at + (1 - core) * half, half)
            copies(own_ref.at[pl.ds(mine, half)], own_ref.at[pl.ds(other, half)], True)

        for other_step in range(1, steps):

            @pl.when(step == other_step)
            def _(other_step=other_step):
                copies(near[other_step - 1], far[other_step - 1], True)

    def end():
        copies(near[0], far[0], False)

    return begin, end


def grad_kernel(steps, at, half, pos_ref, cot_ref, own_ref, *refs):
    near, far = refs[: steps - 1], refs[steps - 1 : 2 * steps - 2]
    outs = refs[2 * steps - 2 : 3 * steps - 2]
    buffer, sems = refs[3 * steps - 2 :]
    group = pos_ref[2]
    ends = []
    for partner in range(steps):
        owner = lax.bitwise_xor(group, partner)
        slot_own = own_ref.at[pl.ds(at, 2 * half)]
        begin, end = fetch_rows(
            pos_ref, slot_own, near, far, buffer, sems, partner, owner, 0, half
        )
        begin()
        ends.append(end)
    for partner in list(range(1, steps)) + [0]:
        ends[partner]()
        outs[partner][...] = lax.dot_general(
            cot_ref[...],
            buffer[partner],
            (((1,), (1,)), ((), ())),
            preferred_element_type=F32,
        ).astype(outs[partner].dtype)


def grad_parts(pos, cotangent, out_w, near, far, at):
    rows, width = cotangent.shape
    steps = len(near) + 1
    half = near[0].shape[0]
    anywhere = pl.BlockSpec(memory_space=pl.ANY)
    return pl.pallas_call(
        functools.partial(grad_kernel, steps, at, half),
        in_specs=[pl.BlockSpec(memory_space=pltpu.SMEM), pl.BlockSpec(memory_space=pltpu.VMEM)]
        + [anywhere] * (2 * steps - 1),
        out_specs=[pl.BlockSpec(memory_space=pltpu.VMEM)] * steps,
        out_shape=[jax.ShapeDtypeStruct((rows, 2 * half), F32)]
        + [jax.ShapeDtypeStruct((rows, 2 * half), BF16)] * (steps - 1),
        scratch_shapes=[
            pltpu.VMEM((steps, 2 * half, width), BF16),
            pltpu.SemaphoreType.DMA((steps, 2)),
        ],
        compiler_params=params(),
        name="grad_parts",
    )(pos, cotangent, out_w, *near, *far)


def out_kernel(steps, pieces, parts, half, pos_ref, own_ref, *refs):
    count = pieces * (steps - 1)
    nears, fars = refs[:count], refs[count : 2 * count]
    gated = refs[2 * count : 2 * count + steps * parts]
    out_ref = refs[2 * count + steps * parts]
    buffers = refs[2 * count + steps * parts + 1 : -2]
    sems, total = refs[-2:]
    group = pos_ref[2]
    ends = {}
    for partner in range(steps):
        owner = lax.bitwise_xor(group, partner)
        for p in range(pieces):
            begin, end = fetch_rows(
                pos_ref,
                own_ref.at[pl.ds(p * 2 * half, 2 * half)],
                nears[p * (steps - 1) : (p + 1) * (steps - 1)],
                fars[p * (steps - 1) : (p + 1) * (steps - 1)],
                buffers[p],
                sems.at[p],
                partner,
                owner,
                0,
                half,
            )
            begin()
            ends[partner, p] = end
    for partner in range(steps):
        for p in range(pieces):
            ends[partner, p]()
        for b in range(parts):
            block = gated[partner * parts + b]
            seqs, rows, width = block.shape
            for p in range(pieces):
                left = block[:, :, p * 2 * half : (p + 1) * 2 * half].reshape(seqs * rows, 2 * half)
                term = jnp.dot(left, buffers[p][partner], preferred_element_type=F32)
                if partner == 0 and p == 0:
                    total[b] = term
                elif partner == steps - 1 and p == pieces - 1:
                    done = (total[b] + term).astype(BF16)
                    for s in range(seqs):
                        out_ref[s, b * rows : (b + 1) * rows] = done[s * rows : (s + 1) * rows]
                else:
                    total[b] += term


def block_output(pos, out_w, nears, fars, gated):
    steps, parts = len(gated), len(gated[0])
    pieces = len(nears)
    half = nears[0][0].shape[0]
    seqs, rows, _ = gated[0][0].shape
    width = out_w.shape[1]
    anywhere = pl.BlockSpec(memory_space=pl.ANY)
    inside = pl.BlockSpec(memory_space=pltpu.VMEM)
    count = pieces * (steps - 1)
    return pl.pallas_call(
        functools.partial(out_kernel, steps, pieces, parts, half),
        in_specs=[pl.BlockSpec(memory_space=pltpu.SMEM)]
        + [anywhere] * (1 + 2 * count)
        + [inside] * (steps * parts),
        out_specs=inside,
        out_shape=jax.ShapeDtypeStruct((seqs, parts * rows, width), BF16),
        scratch_shapes=[pltpu.VMEM((steps, 2 * half, width), BF16)] * pieces
        + [
            pltpu.SemaphoreType.DMA((pieces, steps, 2)),
            pltpu.VMEM((parts, seqs * rows, width), F32),
        ],
        compiler_params=params(48),
        name="block_output",
    )(
        pos,
        out_w,
        *[block for piece in nears for block in piece],
        *[block for piece in fars for block in piece],
        *[block for partner in gated for block in partner],
    )


def mix_grad_kernel(steps, *refs):
    terms = refs[:steps]
    q_ref, low_ref, high_ref, mix_ref, query_ref, pack_ref = refs[steps:]
    seqs, rows = q_ref.shape[0], low_ref.shape[1]
    for s in range(seqs):
        for b, mixed_ref in enumerate((low_ref, high_ref)):
            at = slice(b * rows, (b + 1) * rows)
            total = terms[0][s, at].astype(F32)
            for term in terms[1:]:
                total = total + term[s, at].astype(F32)
            gated_grad = total.astype(BF16).astype(F32)
            mix_ref[s, at] = (gated_grad * q_ref[s, at]).astype(BF16)
            query_ref[s, at] = (gated_grad * mixed_ref[s]).astype(BF16)
        pack_ref[s, :HALO] = mix_ref[s, :HALO]
        pack_ref[s, HALO:] = query_ref[s, :EXTRA]


def mix_grads(terms, query, mixed, offset):
    seqs, rows, width = terms[0].shape
    half = rows // 2
    first = offset // LANES
    local = lambda count: pl.BlockSpec((seqs, count, LANES), lambda i: (0, 0, i))
    wide = lambda count: pl.BlockSpec((seqs, count, LANES), lambda i: (0, 0, first + i))
    return pl.pallas_call(
        functools.partial(mix_grad_kernel, len(terms)),
        grid=(width // LANES,),
        in_specs=[local(rows)] * len(terms) + [wide(rows), wide(half), wide(half)],
        out_specs=[local(rows), local(rows), local(HALO + EXTRA)],
        out_shape=[
            jax.ShapeDtypeStruct((seqs, rows, width), BF16),
            jax.ShapeDtypeStruct((seqs, rows, width), BF16),
            jax.ShapeDtypeStruct((seqs, HALO + EXTRA, width), BF16),
        ],
        compiler_params=params(),
        name="mix_grads",
    )(*terms, query, *mixed)


def filter_kernel(group_size, mix_ref, product_ref, front_ref, out_ref, left, columns):
    seqs = mix_ref.shape[0]
    rows = front_ref.shape[1]
    groups = LANES // group_size
    lane = lax.broadcasted_iota(jnp.int32, (1, LANES), 1) // group_size
    total = None
    for b in range(mix_ref.shape[1] // rows):
        for s in range(seqs):
            at = slice(s * LANES, (s + 1) * LANES)
            block = mix_ref[s, b * rows : (b + 1) * rows]
            for g in range(groups):
                keep = (lane == g).astype(F32).astype(BF16)
                left[b, g * rows : (g + 1) * rows, at] = block * keep
            if b == 0:
                columns[b, :rows, at] = front_ref[s]
            else:
                columns[b, :rows, at] = product_ref[s, (b - 1) * rows : b * rows]
            columns[b, rows:, at] = product_ref[s, b * rows : (b + 1) * rows]
        term = lax.dot_general(
            left[b], columns[b], (((1,), (1,)), ((), ())), preferred_element_type=F32
        )
        total = term if total is None else total + term
    span = 2 * rows
    folded = []
    for g in range(groups):
        sum_g = None
        for a in range(rows // 8):
            tile = total[g * rows + a * 8 : g * rows + a * 8 + 8]
            tile = pltpu.roll(tile, (span - a * 8) % span, 1)
            sum_g = tile if sum_g is None else sum_g + tile
        folded.append(sum_g)
    stacked = jnp.stack(folded, axis=0)
    result = None
    for r in range(8):
        row = pltpu.roll(stacked[:, r, :], (span - r) % span, 1)
        result = row if result is None else result + row
    out_ref[...] = result


def filter_sums(mix_grad, product, front, offset, group_size):
    seqs, rows, width = mix_grad.shape
    block_rows = front.shape[1]
    first = offset // LANES
    groups = LANES // group_size
    blocks = rows // block_rows
    return pl.pallas_call(
        functools.partial(filter_kernel, group_size),
        grid=(width // LANES,),
        in_specs=[
            pl.BlockSpec((seqs, rows, LANES), lambda i: (0, 0, i)),
            pl.BlockSpec((seqs, rows, LANES), lambda i: (0, 0, first + i)),
            pl.BlockSpec((seqs, block_rows, LANES), lambda i: (0, 0, first + i)),
        ],
        out_specs=pl.BlockSpec((groups, 2 * block_rows), lambda i: (i, 0)),
        out_shape=jax.ShapeDtypeStruct((width // group_size, 2 * block_rows), F32),
        scratch_shapes=[
            pltpu.VMEM((blocks, groups * block_rows, seqs * LANES), BF16),
            pltpu.VMEM((blocks, 2 * block_rows, seqs * LANES), BF16),
        ],
        compiler_params=params(),
        name="filter_sums",
    )(mix_grad, product, front)


def input_grad_kernel(
    group_size,
    line_ref,
    mix_ref,
    query_ref,
    back_ref,
    k_ref,
    v_ref,
    x_ref,
    front_ref,
    next_ref,
    w_ref,
    out_ref,
    sums_ref,
    band,
    columns,
    grads,
    inputs,
    edge,
):
    seqs, rows = mix_ref.shape[0], mix_ref.shape[1]
    block = line_ref.shape[1] // 2
    groups = LANES // group_size
    fill_band(line_ref, band, block)
    found = []
    for b in range(rows // block):
        for s in range(seqs):
            at = slice(s * LANES, (s + 1) * LANES)
            columns[b, :block, at] = mix_ref[s, b * block : (b + 1) * block]
            if (b + 1) * block < rows:
                columns[b, block:, at] = mix_ref[s, (b + 1) * block : (b + 2) * block]
            else:
                columns[b, block:, at] = back_ref[s, :block]
        stacked = jnp.dot(band[...], columns[b], preferred_element_type=F32)
        found.append(pick_groups(stacked, block, group_size))
    last = rows // block
    for s in range(seqs):
        at = slice(s * LANES, (s + 1) * LANES)
        columns[last, :HALO, at] = back_ref[s, :HALO]
        columns[last, HALO:, at] = jnp.zeros((2 * block - HALO, LANES), BF16)
    few = jnp.concatenate([band[g * block : g * block + EXTRA] for g in range(groups)], axis=0)
    stacked = jnp.dot(few, columns[last], preferred_element_type=F32)
    beyond = pick_groups(stacked, EXTRA, group_size)
    for s in range(seqs):
        at = slice(s * LANES, (s + 1) * LANES)
        after = []
        for j in (1, 2):
            own = s * 2 + j - 1
            edge[own, 0:8] = x_ref[j, s, rows - 16 :].astype(F32)[8:]
            edge[own, 8:16] = next_ref[j - 1, s]
            total = w_ref[j, 0:1] * edge[own, 8:16]
            total = total + w_ref[j, 1:2] * edge[own, 7:15]
            total = total + w_ref[j, 2:3] * edge[own, 6:14]
            after.append(total)
        for j in range(3):
            own = s * 3 + j
            if j == 0:
                grads[own, :rows] = query_ref[s].astype(F32)
                grads[own, rows:] = back_ref[s, HALO:].astype(F32)[:8]
            else:
                factor_ref = v_ref if j == 1 else k_ref
                for b in range(rows // block):
                    part = slice(b * block, (b + 1) * block)
                    value = found[b][:, at] * factor_ref[s, part]
                    grads[own, part] = value.astype(BF16).astype(F32)
                value = beyond[:8, at] * after[2 - j]
                grads[own, rows:] = value.astype(BF16).astype(F32)
            inputs[own, 0:8] = front_ref[j, s]
            inputs[own, 8 : 8 + rows] = x_ref[j, s].astype(F32)
            total = None
            for i in range(3):
                term = w_ref[j, i : i + 1] * grads[own, i : i + rows]
                total = term if total is None else total + term
            out_ref[j, s] = total.astype(BF16)
    for j in range(3):
        for i in range(3):
            total = None
            for s in range(seqs):
                own = s * 3 + j
                term = grads[own, :rows] * inputs[own, 8 - i : 8 - i + rows]
                term = jnp.sum(term, axis=0, keepdims=True)
                total = term if total is None else total + term
            sums_ref[j * 3 + i : j * 3 + i + 1] = total


def input_grads(line, mix_grad, query_grad, back, keys, values, x, front, following, short_w, offset, group_size):
    seqs, rows, width = mix_grad.shape
    block = line.shape[1] // 2
    first = offset // LANES
    groups = LANES // group_size
    local = lambda count: pl.BlockSpec((seqs, count, LANES), lambda i: (0, 0, i))
    wide3 = lambda *sizes: pl.BlockSpec(sizes + (LANES,), lambda i: (0, 0, first + i))
    wide4 = lambda *sizes: pl.BlockSpec(sizes + (LANES,), lambda i: (0, 0, 0, first + i))
    return pl.pallas_call(
        functools.partial(input_grad_kernel, group_size),
        grid=(width // LANES,),
        in_specs=[
            pl.BlockSpec((groups, 2 * block), lambda i: (first + i, 0)),
            local(rows),
            local(rows),
            local(HALO + EXTRA),
            wide3(seqs, rows),
            wide3(seqs, rows),
            wide4(3, seqs, rows),
            wide4(3, seqs, 8),
            wide4(2, seqs, 8),
            wide3(3, 3),
        ],
        out_specs=[
            pl.BlockSpec((3, seqs, rows, LANES), lambda i: (0, 0, 0, i)),
            pl.BlockSpec((9, LANES), lambda i: (0, i)),
        ],
        out_shape=[
            jax.ShapeDtypeStruct((3, seqs, rows, width), BF16),
            jax.ShapeDtypeStruct((9, width), F32),
        ],
        scratch_shapes=[
            pltpu.VMEM((groups * block, 2 * block), BF16),
            pltpu.VMEM((rows // block + 1, 2 * block, seqs * LANES), BF16),
            pltpu.VMEM((3 * seqs, rows + 8, LANES), F32),
            pltpu.VMEM((3 * seqs, rows + 8, LANES), F32),
            pltpu.VMEM((2 * seqs, 16, LANES), F32),
        ],
        compiler_params=params(),
        name="input_grads",
    )(line, mix_grad, query_grad, back, keys, values, x, front, following, short_w)


def chain(pieces, axis):
    count = lax.axis_size(axis)
    here = lax.axis_index(axis)
    up = [[piece] for piece in pieces]
    down = [[piece] for piece in pieces]
    for step in range(1, count):
        for p in range(len(pieces)):
            up[p].append(shift(up[p][-1], axis, 1, step - 1))
            down[p].append(shift(down[p][-1], axis, -1, step - 1))
    return [
        [jnp.where(here >= s, up[p][s], down[p][count - s]) for s in range(1, count)]
        for p in range(len(pieces))
    ]


def total_over(block, axes):
    count = math.prod(lax.axis_size(axis) for axis in axes)
    if count & (count - 1):
        return lax.psum(block, axes)
    step = count // 2
    order = []
    while step:
        order.append(step)
        step //= 2
    for step in order:
        block = block + lax.ppermute(block, axes, [(i, i ^ step) for i in range(count)])
    return block


def shards(projected, short_w, medium_h, out_w, grad_out):
    seqs, rows, _, width = projected.shape
    taps = medium_h.shape[1]
    group_size = width // medium_h.shape[0]
    members = lax.axis_size("grp")
    cores = lax.axis_size("dp")
    partners = range(members)
    to = lambda block, k: lax.ppermute(block, "grp", [(i, i ^ k) for i in partners])
    pos = jnp.stack([lax.axis_index("ctx"), lax.axis_index("dp"), lax.axis_index("grp")])
    pos = pos.astype(jnp.int32)
    ring = out_w.shape[0] == width and lax.axis_size("ctx") == members and cores == 2
    pieces = 2 if ring else 1
    span = width // pieces

    if ring:
        half = span // 2
        core = lax.axis_index("dp")
        sent = [
            lax.dynamic_slice_in_dim(out_w, p * span + core * half, half, axis=0)
            for p in range(pieces)
        ]
        near = chain(sent, "ctx")
        far = [[lax.ppermute(block, "dp", [(0, 1), (1, 0)]) for block in piece] for piece in near]

    x = jnp.transpose(projected, (2, 0, 1, 3))
    front = shift(x[:, :, rows - 2 :], "ctx", 1).astype(F32)
    front = jnp.pad(front, ((0, 0), (0, 0), (6, 0), (0, 0)))
    following = shift(x[1:, :, :2], "ctx", -1).astype(F32)
    following = jnp.pad(following, ((0, 0), (0, 0), (0, 6), (0, 0)))
    filters = medium_h.astype(F32)
    empty = jnp.zeros_like(filters)
    causal = jnp.concatenate([empty[:, :1], filters[:, ::-1], empty[:, 1:]], axis=1)
    anticausal = jnp.concatenate([filters, empty], axis=1)

    product, query, keys, values = features(x, front, short_w)
    product_front = shift(product[:, rows - taps :], "ctx", 1)
    mixed_high, gated_high = mix(causal, product, 0, product, 1, query, 1, taps, group_size)
    mixed_low, gated_low = mix(causal, product_front, 0, product, 0, query, 0, taps, group_size)
    gated = [[gated_low, gated_high]]
    for k in partners[1:]:
        gated.append([to(gated_low, k), to(gated_high, k)])

    cotangent = grad_out.reshape(seqs * rows, width)
    if not ring:
        whole_w = lax.all_gather(out_w, "ctx", axis=0, tiled=True)
        own = lax.axis_index("grp")
        blocks = [
            lax.dynamic_slice_in_dim(whole_w, lax.bitwise_xor(own, k) * width, width, axis=0)
            for k in partners
        ]

    outs, sums = [], []
    for p in range(pieces):
        if ring:
            parts = grad_parts(pos, cotangent, out_w, near[p], far[p], p * span)
        else:
            parts = [
                lax.dot_general(
                    cotangent, block, (((1,), (1,)), ((), ())), preferred_element_type=F32
                ).astype(F32 if k == 0 else BF16)
                for k, block in enumerate(blocks)
            ]
        terms = [parts[0]] + [to(parts[k], k) for k in partners[1:]]
        terms = [term.reshape(seqs, rows, span) for term in terms]
        mix_grad, query_grad, pack = mix_grads(terms, query, (mixed_low, mixed_high), p * span)
        back = shift(pack, "ctx", -1)
        folded = filter_sums(mix_grad, product, product_front, p * span, group_size)
        grad, short = input_grads(
            anticausal,
            mix_grad,
            query_grad,
            back,
            keys,
            values,
            x,
            front,
            following,
            short_w,
            p * span,
            group_size,
        )
        outs.append(grad)
        flat = jnp.concatenate(
            [folded[:, 1 : taps + 1].reshape(-1, LANES), short.reshape(-1, LANES)], axis=0
        )
        sums.append(total_over(flat, ("dp", "ctx")))

    if ring:
        block_out = block_output(pos, out_w, near, far, gated)
    else:
        total = None
        for k in partners:
            left = jnp.concatenate(gated[k], axis=1).reshape(seqs * rows, width)
            term = jnp.dot(left, blocks[k], preferred_element_type=F32)
            total = term if total is None else total + term
        block_out = total.astype(BF16).reshape(seqs, rows, width)

    grad_projected = jnp.transpose(jnp.concatenate(outs, axis=3), (1, 2, 0, 3))
    group_rows = span // group_size * taps // LANES
    filter_total = jnp.concatenate(
        [part[:group_rows].reshape(-1, taps) for part in sums], axis=0
    )[:, ::-1]
    short_total = jnp.concatenate(
        [part[group_rows:].reshape(3, 3, span) for part in sums], axis=2
    )
    seq_total = seqs * cores
    length_total = rows * lax.axis_size("ctx")
    filter_grad = filter_total / math.sqrt(seq_total * length_total * group_size)
    short_grad = short_total / math.sqrt(seq_total * length_total)
    return (block_out, grad_projected, filter_grad, short_grad)


def solution(mesh):
    in_specs = (
        P("dp", "ctx", None, "grp"),
        P(None, None, "grp"),
        P("grp", None),
        P("ctx", "grp"),
        P("dp", "ctx", "grp"),
    )
    out_specs = (
        P("dp", "ctx", "grp"),
        P("dp", "ctx", None, "grp"),
        P("grp", None),
        P(None, None, "grp"),
    )
    return jax.shard_map(shards, mesh=mesh, in_specs=in_specs, out_specs=out_specs, check_vma=False)
```

```python
import functools
import math

import jax
import jax.numpy as jnp
from jax import lax
from jax.experimental import pallas as pl
from jax.experimental.pallas import tpu as pltpu
from jax.sharding import PartitionSpec as P

LANES = 128
HALO = 144
FIRST = 3
EXTRA = 16
F32 = jnp.float32
BF16 = jnp.bfloat16


def params(mib=24):
    return pltpu.CompilerParams(vmem_limit_bytes=mib * 1024 * 1024)


def shift(block, axis, distance):
    devices = range(lax.axis_size(axis))
    route = [(i, i + distance) for i in devices if i + distance in devices]
    return lax.ppermute(block, axis, route)


def after(block, *others):
    return lax.optimization_barrier((block, *others))[0]


def pick_groups(stacked, rows, group_size):
    width = stacked.shape[1]
    lane = lax.broadcasted_iota(jnp.int32, (1, width), 1) % LANES
    groups = LANES // group_size
    total = stacked[:rows]
    for g in range(1, groups):
        total = jnp.where(lane >= g * group_size, stacked[g * rows : (g + 1) * rows], total)
    return total


def fill_band(line_ref, band_ref, rows):
    for g in range(line_ref.shape[0]):
        wide = jnp.broadcast_to(line_ref[g : g + 1, :], (rows, line_ref.shape[1]))
        moved = pltpu.roll(wide, 0, 1, stride=1, stride_axis=0)
        band_ref[g * rows : (g + 1) * rows, :] = moved.astype(BF16)


def convolve(x_ref, w_ref, pad, j, s, head):
    rows = x_ref.shape[2]
    own = s * 3 + j
    pad[own, 0:8] = head
    pad[own, 8 : 8 + rows] = x_ref[j, s].astype(F32)
    total = w_ref[j, 0:1] * pad[own, 8 : 8 + rows]
    total = total + w_ref[j, 1:2] * pad[own, 7 : 7 + rows]
    return total + w_ref[j, 2:3] * pad[own, 6 : 6 + rows]


def front_rows(front_ref, j, s, taps):
    return front_ref[s, taps : taps + 2 * EXTRA].astype(F32)[j * 8 : j * 8 + 8]


def product_kernel(x_ref, w_ref, product_ref, pack_ref, pad):
    seqs, rows = x_ref.shape[1], x_ref.shape[2]
    taps = pack_ref.shape[1] - 2 * EXTRA
    nothing = jnp.zeros((8, LANES), F32)
    for s in range(seqs):
        keys = convolve(x_ref, w_ref, pad, 1, s, nothing)
        values = convolve(x_ref, w_ref, pad, 2, s, nothing)
        product = (keys * values).astype(BF16)
        product_ref[s] = product
        pack_ref[s, :taps] = product[rows - taps :]
        tails = [x_ref[j, s, rows - 16 :].astype(F32)[8:] for j in range(3)]
        pack_ref[s, taps:] = jnp.concatenate(tails + [nothing], axis=0).astype(BF16)


def products(x, short_w, taps):
    _, seqs, rows, width = x.shape
    at3 = lambda i: (0, 0, i)
    return pl.pallas_call(
        product_kernel,
        grid=(width // LANES,),
        in_specs=[
            pl.BlockSpec((3, seqs, rows, LANES), lambda i: (0, 0, 0, i)),
            pl.BlockSpec((3, 3, LANES), at3),
        ],
        out_specs=[
            pl.BlockSpec((seqs, rows, LANES), at3),
            pl.BlockSpec((seqs, taps + 2 * EXTRA, LANES), at3),
        ],
        out_shape=[
            jax.ShapeDtypeStruct((seqs, rows, width), BF16),
            jax.ShapeDtypeStruct((seqs, taps + 2 * EXTRA, width), BF16),
        ],
        scratch_shapes=[pltpu.VMEM((3 * seqs, rows + 8, LANES), F32)],
        compiler_params=params(),
        name="products",
    )(x, short_w)


def mix_high_kernel(
    group_size, line_ref, low_ref, high_ref, x_ref, w_ref, mixed_ref, gated_ref, band, columns, pad
):
    seqs, rows = low_ref.shape[0], low_ref.shape[1]
    fill_band(line_ref, band, rows)
    for s in range(seqs):
        at = slice(s * LANES, (s + 1) * LANES)
        columns[:rows, at] = low_ref[s]
        columns[rows:, at] = high_ref[s]
    stacked = jnp.dot(band[...], columns[...], preferred_element_type=F32)
    mixed = pick_groups(stacked, rows, group_size)
    nothing = jnp.zeros((8, LANES), F32)
    for s in range(seqs):
        part = mixed[:, s * LANES : (s + 1) * LANES]
        mixed_ref[s] = part
        query = convolve(x_ref, w_ref, pad, 0, s, nothing)[rows:]
        gated_ref[s] = (query * part).astype(BF16)


def mix_high(line, product, x, short_w, rows, group_size):
    _, seqs, length, width = x.shape
    groups = LANES // group_size
    part = lambda at: pl.BlockSpec((seqs, rows, LANES), lambda i: (0, at, i))
    shape = (seqs, rows, width)
    return pl.pallas_call(
        functools.partial(mix_high_kernel, group_size),
        grid=(width // LANES,),
        in_specs=[
            pl.BlockSpec((groups, 2 * rows), lambda i: (i, 0)),
            part(0),
            part(1),
            pl.BlockSpec((1, seqs, length, LANES), lambda i: (0, 0, 0, i)),
            pl.BlockSpec((3, 3, LANES), lambda i: (0, 0, i)),
        ],
        out_specs=[part(0), part(0)],
        out_shape=[jax.ShapeDtypeStruct(shape, F32), jax.ShapeDtypeStruct(shape, BF16)],
        scratch_shapes=[
            pltpu.VMEM((groups * rows, 2 * rows), BF16),
            pltpu.VMEM((2 * rows, seqs * LANES), BF16),
            pltpu.VMEM((3 * seqs, length + 8, LANES), F32),
        ],
        compiler_params=params(),
        name="mix_high",
    )(line, product, product, x, short_w)


def mix_low_kernel(
    group_size,
    line_ref,
    front_ref,
    product_ref,
    x_ref,
    w_ref,
    mixed_ref,
    gated_ref,
    head_ref,
    band,
    columns,
    pad,
):
    seqs, rows = product_ref.shape[0], product_ref.shape[1]
    fill_band(line_ref, band, rows)
    queries = []
    for s in range(seqs):
        at = slice(s * LANES, (s + 1) * LANES)
        found = [
            convolve(x_ref, w_ref, pad, j, s, front_rows(front_ref, j, s, rows)) for j in range(3)
        ]
        queries.append(found[0])
        head = (found[1][:EXTRA] * found[2][:EXTRA]).astype(BF16)
        head_ref[s] = head
        columns[:rows, at] = front_ref[s, :rows]
        columns[rows : rows + EXTRA, at] = head
        columns[rows + EXTRA :, at] = product_ref[s, EXTRA:]
    stacked = jnp.dot(band[...], columns[...], preferred_element_type=F32)
    mixed = pick_groups(stacked, rows, group_size)
    for s in range(seqs):
        part = mixed[:, s * LANES : (s + 1) * LANES]
        mixed_ref[s] = part
        gated_ref[s] = (queries[s] * part).astype(BF16)


def mix_low(line, front, product, x, short_w, rows, group_size):
    _, seqs, _, width = x.shape
    groups = LANES // group_size
    part = lambda count: pl.BlockSpec((seqs, count, LANES), lambda i: (0, 0, i))
    shape = (seqs, rows, width)
    return pl.pallas_call(
        functools.partial(mix_low_kernel, group_size),
        grid=(width // LANES,),
        in_specs=[
            pl.BlockSpec((groups, 2 * rows), lambda i: (i, 0)),
            part(front.shape[1]),
            part(rows),
            pl.BlockSpec((3, seqs, rows, LANES), lambda i: (0, 0, 0, i)),
            pl.BlockSpec((3, 3, LANES), lambda i: (0, 0, i)),
        ],
        out_specs=[part(rows), part(rows), part(EXTRA)],
        out_shape=[
            jax.ShapeDtypeStruct(shape, F32),
            jax.ShapeDtypeStruct(shape, BF16),
            jax.ShapeDtypeStruct((seqs, EXTRA, width), BF16),
        ],
        scratch_shapes=[
            pltpu.VMEM((groups * rows, 2 * rows), BF16),
            pltpu.VMEM((2 * rows, seqs * LANES), BF16),
            pltpu.VMEM((3 * seqs, rows + 8, LANES), F32),
        ],
        compiler_params=params(),
        name="mix_low",
    )(line, front, product, x, short_w)


class Gathered:
    def __init__(self, w, steps, start):
        self.arrays, self.start, self.span = [w], start, w.shape[0] // steps

    def fetch(self, pos_ref, refs, buffer, base, sems, partner):
        owner = lax.bitwise_xor(pos_ref[2], partner)
        rows = pl.ds(pl.multiple_of(owner * self.span, self.span), self.span)
        place = buffer.at[partner, pl.ds(base, self.span)]
        copy = pltpu.make_async_copy(refs[0].at[rows], place, sems.at[partner, 0])
        copy.start()
        return [copy]


class Passed:
    def __init__(self, own, near, far, start):
        self.arrays, self.start, self.span = [own, *near, *far], start, 2 * near[0].shape[0]

    def fetch(self, pos_ref, refs, buffer, base, sems, partner):
        steps, half = (len(refs) + 1) // 2, self.span // 2
        owner = lax.bitwise_xor(pos_ref[2], partner)
        step = lax.rem(pos_ref[0] - owner + steps, steps)
        mine = pl.multiple_of(pos_ref[1] * half, half)
        other = pl.multiple_of((1 - pos_ref[1]) * half, half)

        def copies(first, second):
            return [
                pltpu.make_async_copy(
                    source, buffer.at[partner, pl.ds(base + place, half)], sems.at[partner, which]
                )
                for which, (source, place) in enumerate(((first, mine), (second, other)))
            ]

        for distance in range(steps):

            @pl.when(step == distance)
            def _(distance=distance):
                if distance == 0:
                    pair = [refs[0].at[pl.ds(self.start + at, half)] for at in (mine, other)]
                else:
                    pair = [refs[distance], refs[steps - 1 + distance]]
                for copy in copies(*pair):
                    copy.start()

        return copies(refs[1], refs[steps])


def grad_kernel(weights, steps, pos_ref, cot_ref, *refs):
    held = len(weights.arrays)
    outs, (buffer, sems) = refs[held : held + steps], refs[held + steps :]
    order = list(range(1, steps)) + [0]
    copies = {
        partner: weights.fetch(pos_ref, refs[:held], buffer, 0, sems, partner)
        for partner in order
    }
    for partner in order:
        for copy in copies[partner]:
            copy.wait()
        outs[partner][...] = lax.dot_general(
            cot_ref[...],
            buffer[partner],
            (((1,), (1,)), ((), ())),
            preferred_element_type=F32,
        ).astype(outs[partner].dtype)


def grad_parts(pos, cotangent, weights, steps):
    rows, width = cotangent.shape
    span = weights.span
    inside = pl.BlockSpec(memory_space=pltpu.VMEM)
    return pl.pallas_call(
        functools.partial(grad_kernel, weights, steps),
        in_specs=[pl.BlockSpec(memory_space=pltpu.SMEM), inside]
        + [pl.BlockSpec(memory_space=pl.ANY)] * len(weights.arrays),
        out_specs=[inside] * steps,
        out_shape=[jax.ShapeDtypeStruct((rows, span), F32)]
        + [jax.ShapeDtypeStruct((rows, span), BF16)] * (steps - 1),
        scratch_shapes=[
            pltpu.VMEM((steps, span, width), BF16),
            pltpu.SemaphoreType.DMA((steps, 2)),
        ],
        compiler_params=params(56),
        name="grad_parts",
    )(pos, cotangent, *weights.arrays)


def out_kernel(weights, steps, pos_ref, *refs):
    out_ref, buffer, *sems = refs[-2 - len(weights) :]
    copies = {partner: [] for partner in range(steps)}
    for piece, piece_sems in zip(weights, sems):
        held, refs = refs[: len(piece.arrays)], refs[len(piece.arrays) :]
        for partner in range(steps):
            copies[partner] += piece.fetch(
                pos_ref, held, buffer, piece.start, piece_sems, partner
            )
    total = None
    for partner in range(steps):
        for copy in copies[partner]:
            copy.wait()
        left = refs[partner][...].reshape(-1, buffer.shape[1])
        term = jnp.dot(left, buffer[partner], preferred_element_type=F32)
        total = term if total is None else total + term
    out_ref[...] = total.astype(BF16).reshape(out_ref.shape)


def block_output(pos, weights, gated, at, blocks, before):
    steps = len(gated)
    seqs, rows, depth = gated[0].shape
    width = weights[0].arrays[0].shape[1]
    inside = pl.BlockSpec(memory_space=pltpu.VMEM)
    anywhere = pl.BlockSpec(memory_space=pl.ANY)
    arrays = [array for piece in weights for array in piece.arrays]
    before = [] if before is None else [before]
    return pl.pallas_call(
        functools.partial(out_kernel, weights, steps),
        grid=(1,),
        in_specs=[pl.BlockSpec(memory_space=pltpu.SMEM)]
        + [anywhere] * len(arrays)
        + [inside] * steps
        + [anywhere] * len(before),
        out_specs=pl.BlockSpec((seqs, rows, width), lambda i: (0, at, 0)),
        out_shape=jax.ShapeDtypeStruct((seqs, blocks * rows, width), BF16),
        scratch_shapes=[pltpu.VMEM((steps, depth, width), BF16)]
        + [pltpu.SemaphoreType.DMA((steps, 2))] * len(weights),
        input_output_aliases={1 + len(arrays) + steps: 0} if before else {},
        compiler_params=params(56),
        name="block_output",
    )(pos, *arrays, *gated, *before)


def mix_grad_kernel(steps, *refs):
    terms = refs[:steps]
    low_ref, high_ref, x_ref, front_ref, w_ref, mix_ref, query_ref, pack_ref, pad = refs[steps:]
    seqs, rows = x_ref.shape[1], low_ref.shape[1]
    for s in range(seqs):
        query = convolve(x_ref, w_ref, pad, 0, s, front_rows(front_ref, 0, s, rows))
        for b, mixed_ref in enumerate((low_ref, high_ref)):
            at = slice(b * rows, (b + 1) * rows)
            total = terms[0][s, at].astype(F32)
            for term in terms[1:]:
                total = total + term[s, at].astype(F32)
            gated_grad = total.astype(BF16).astype(F32)
            mix_ref[s, at] = (gated_grad * query[at]).astype(BF16)
            query_ref[s, at] = (gated_grad * mixed_ref[s]).astype(BF16)
        pack_ref[s, :HALO] = mix_ref[s, :HALO]
        pack_ref[s, HALO : HALO + EXTRA] = query_ref[s, :EXTRA]
        heads = [x_ref[j, s, :EXTRA].astype(F32)[:8] for j in (1, 2)]
        pack_ref[s, HALO + EXTRA :] = jnp.concatenate(heads, axis=0).astype(BF16)


def mix_grads(terms, mixed, x, front, short_w, offset):
    seqs, rows, width = terms[0].shape
    half = rows // 2
    first = offset // LANES
    local = lambda count: pl.BlockSpec((seqs, count, LANES), lambda i: (0, 0, i))
    wide = lambda count: pl.BlockSpec((seqs, count, LANES), lambda i: (0, 0, first + i))
    return pl.pallas_call(
        functools.partial(mix_grad_kernel, len(terms)),
        grid=(width // LANES,),
        in_specs=[local(rows)] * len(terms)
        + [wide(half), wide(half)]
        + [
            pl.BlockSpec((3, seqs, rows, LANES), lambda i: (0, 0, 0, first + i)),
            wide(front.shape[1]),
            pl.BlockSpec((3, 3, LANES), lambda i: (0, 0, first + i)),
        ],
        out_specs=[local(rows), local(rows), local(HALO + 2 * EXTRA)],
        out_shape=[
            jax.ShapeDtypeStruct((seqs, rows, width), BF16),
            jax.ShapeDtypeStruct((seqs, rows, width), BF16),
            jax.ShapeDtypeStruct((seqs, HALO + 2 * EXTRA, width), BF16),
        ],
        scratch_shapes=[pltpu.VMEM((3 * seqs, rows + 8, LANES), F32)],
        compiler_params=params(),
        name="mix_grads",
    )(*terms, *mixed, x, front, short_w)


def filter_kernel(
    group_size, mix_ref, product_ref, head_ref, front_ref, out_ref, left, columns
):
    seqs = mix_ref.shape[0]
    rows = out_ref.shape[1]
    groups = LANES // group_size
    lane = lax.broadcasted_iota(jnp.int32, (1, LANES), 1) // group_size
    total = None
    for b in range(mix_ref.shape[1] // rows):
        for s in range(seqs):
            at = slice(s * LANES, (s + 1) * LANES)
            block = mix_ref[s, b * rows : (b + 1) * rows]
            for g in range(groups):
                keep = (lane == g).astype(F32).astype(BF16)
                left[b, g * rows : (g + 1) * rows, at] = block * keep
            if b == 0:
                columns[b, :rows, at] = front_ref[s, :rows]
            else:
                columns[b, :rows, at] = product_ref[s, (b - 1) * rows : b * rows]
            columns[b, rows:, at] = product_ref[s, b * rows : (b + 1) * rows]
            if b < 2:
                start = (1 - b) * rows
                columns[b, start : start + EXTRA, at] = head_ref[s]
        term = lax.dot_general(
            left[b], columns[b], (((1,), (1,)), ((), ())), preferred_element_type=F32
        )
        total = term if total is None else total + term
    span = 2 * rows
    folded = []
    for g in range(groups):
        sum_g = None
        for a in range(rows // 8):
            tile = total[g * rows + a * 8 : g * rows + a * 8 + 8]
            tile = pltpu.roll(tile, (span - a * 8) % span, 1)
            sum_g = tile if sum_g is None else sum_g + tile
        folded.append(sum_g)
    stacked = jnp.stack(folded, axis=0)
    result = None
    for r in range(8):
        row = pltpu.roll(stacked[:, r, :], span - r - 1, 1)
        result = row if result is None else result + row
    out_ref[...] = result[:, :rows]


def filter_sums(mix_grad, product, head, front, block_rows, offset, group_size):
    seqs, rows, width = mix_grad.shape
    first = offset // LANES
    groups = LANES // group_size
    blocks = rows // block_rows
    return pl.pallas_call(
        functools.partial(filter_kernel, group_size),
        grid=(width // LANES,),
        in_specs=[
            pl.BlockSpec((seqs, rows, LANES), lambda i: (0, 0, i)),
            pl.BlockSpec((seqs, rows, LANES), lambda i: (0, 0, first + i)),
            pl.BlockSpec((seqs, EXTRA, LANES), lambda i: (0, 0, first + i)),
            pl.BlockSpec((seqs, front.shape[1], LANES), lambda i: (0, 0, first + i)),
        ],
        out_specs=pl.BlockSpec((groups, block_rows), lambda i: (i, 0)),
        out_shape=jax.ShapeDtypeStruct((width // group_size, block_rows), F32),
        scratch_shapes=[
            pltpu.VMEM((blocks, groups * block_rows, seqs * LANES), BF16),
            pltpu.VMEM((blocks, 2 * block_rows, seqs * LANES), BF16),
        ],
        compiler_params=params(),
        name="filter_sums",
    )(mix_grad, product, head, front)


def input_grad_kernel(
    group_size,
    line_ref,
    mix_ref,
    query_ref,
    back_ref,
    x_ref,
    front_ref,
    w_ref,
    filter_ref,
    out_ref,
    sums_ref,
    band,
    columns,
    grads,
    inputs,
    edge,
):
    seqs, rows = mix_ref.shape[0], mix_ref.shape[1]
    block = line_ref.shape[1] // 2
    groups = LANES // group_size
    fill_band(line_ref, band, block)
    found = []
    for b in range(rows // block):
        for s in range(seqs):
            at = slice(s * LANES, (s + 1) * LANES)
            columns[b, :block, at] = mix_ref[s, b * block : (b + 1) * block]
            if (b + 1) * block < rows:
                columns[b, block:, at] = mix_ref[s, (b + 1) * block : (b + 2) * block]
            else:
                columns[b, block:, at] = back_ref[s, :block]
        stacked = jnp.dot(band[...], columns[b], preferred_element_type=F32)
        found.append(pick_groups(stacked, block, group_size))
    last = rows // block
    for s in range(seqs):
        at = slice(s * LANES, (s + 1) * LANES)
        columns[last, :HALO, at] = back_ref[s, :HALO]
        columns[last, HALO:, at] = jnp.zeros((2 * block - HALO, LANES), BF16)
    few = jnp.concatenate([band[g * block : g * block + EXTRA] for g in range(groups)], axis=0)
    stacked = jnp.dot(few, columns[last], preferred_element_type=F32)
    beyond = pick_groups(stacked, EXTRA, group_size)
    for s in range(seqs):
        at = slice(s * LANES, (s + 1) * LANES)
        after = []
        for j in (1, 2):
            own = s * 2 + j - 1
            edge[own, 0:8] = x_ref[j, s, rows - 16 :].astype(F32)[8:]
            edge[own, 8:16] = back_ref[s, HALO + EXTRA :].astype(F32)[8 * j - 8 : 8 * j]
            total = w_ref[j, 0:1] * edge[own, 8:16]
            total = total + w_ref[j, 1:2] * edge[own, 7:15]
            total = total + w_ref[j, 2:3] * edge[own, 6:14]
            after.append(total)
        streams = [
            convolve(x_ref, w_ref, inputs, j, s, front_rows(front_ref, j, s, block))
            for j in range(1, 3)
        ]
        inputs[s * 3, 0:8] = front_rows(front_ref, 0, s, block)
        inputs[s * 3, 8 : 8 + rows] = x_ref[0, s].astype(F32)
        for j in range(3):
            own = s * 3 + j
            if j == 0:
                grads[own, :rows] = query_ref[s].astype(F32)
                grads[own, rows:] = back_ref[s, HALO : HALO + EXTRA].astype(F32)[:8]
            else:
                factor = streams[2 - j]
                for b in range(rows // block):
                    part = slice(b * block, (b + 1) * block)
                    value = found[b][:, at] * factor[part]
                    grads[own, part] = value.astype(BF16).astype(F32)
                value = beyond[:8, at] * after[2 - j]
                grads[own, rows:] = value.astype(BF16).astype(F32)
            total = None
            for i in range(3):
                term = w_ref[j, i : i + 1] * grads[own, i : i + rows]
                total = term if total is None else total + term
            out_ref[j, s] = total.astype(BF16)
    for j in range(3):
        for i in range(3):
            total = None
            for s in range(seqs):
                own = s * 3 + j
                term = grads[own, :rows] * inputs[own, 8 - i : 8 - i + rows]
                term = jnp.sum(term, axis=0, keepdims=True)
                total = term if total is None else total + term
            sums_ref[0, groups + j * 3 + i : groups + j * 3 + i + 1] = total
    sums_ref[0, :groups] = filter_ref[...]
    sums_ref[0, groups + 9 :] = jnp.zeros((sums_ref.shape[1] - groups - 9, LANES), F32)


def input_grads(
    line, mix_grad, query_grad, back, x, front, short_w, filter_part, offset, group_size
):
    seqs, rows, width = mix_grad.shape
    block = line.shape[1] // 2
    first = offset // LANES
    groups = LANES // group_size
    local = lambda count: pl.BlockSpec((seqs, count, LANES), lambda i: (0, 0, i))
    wide3 = lambda *sizes: pl.BlockSpec(sizes + (LANES,), lambda i: (0, 0, first + i))
    wide4 = lambda *sizes: pl.BlockSpec(sizes + (LANES,), lambda i: (0, 0, 0, first + i))
    return pl.pallas_call(
        functools.partial(input_grad_kernel, group_size),
        grid=(width // LANES,),
        in_specs=[
            pl.BlockSpec((groups, 2 * block), lambda i: (first + i, 0)),
            local(rows),
            local(rows),
            local(HALO + 2 * EXTRA),
            wide4(3, seqs, rows),
            wide3(seqs, front.shape[1]),
            wide3(3, 3),
            pl.BlockSpec((groups, block), lambda i: (i, 0)),
        ],
        out_specs=[
            pl.BlockSpec((3, seqs, rows, LANES), lambda i: (0, 0, 0, i)),
            pl.BlockSpec((1, groups + 16, LANES), lambda i: (i, 0, 0)),
        ],
        out_shape=[
            jax.ShapeDtypeStruct((3, seqs, rows, width), BF16),
            jax.ShapeDtypeStruct((width // LANES, groups + 16, LANES), F32),
        ],
        scratch_shapes=[
            pltpu.VMEM((groups * block, 2 * block), BF16),
            pltpu.VMEM((rows // block + 1, 2 * block, seqs * LANES), BF16),
            pltpu.VMEM((3 * seqs, rows + 8, LANES), F32),
            pltpu.VMEM((3 * seqs, rows + 8, LANES), F32),
            pltpu.VMEM((2 * seqs, 16, LANES), F32),
        ],
        compiler_params=params(),
        name="input_grads",
    )(line, mix_grad, query_grad, back, x, front, short_w, filter_part)


def total_over(block, axes):
    count = math.prod(lax.axis_size(axis) for axis in axes)
    if count & (count - 1):
        return lax.psum(block, axes)
    step = count // 2
    order = []
    while step:
        order.append(step)
        step //= 2
    for step in order:
        block = block + lax.ppermute(block, axes, [(i, i ^ step) for i in range(count)])
    return block


def shards(projected, short_w, medium_h, out_w, grad_out):
    seqs, rows, _, width = projected.shape
    taps = medium_h.shape[1]
    group_size = width // medium_h.shape[0]
    groups = LANES // group_size
    members = lax.axis_size("grp")
    cores = lax.axis_size("dp")
    length = lax.axis_size("ctx")
    partners = range(members)
    to = lambda block, k: lax.ppermute(block, "grp", [(i, i ^ k) for i in partners])
    around = lambda block: lax.ppermute(block, "ctx", [(i, (i + 1) % length) for i in range(length)])
    swap = lambda block: lax.ppermute(block, "dp", [(0, 1), (1, 0)])
    core = lax.axis_index("dp")
    pos = jnp.stack([lax.axis_index("ctx"), core, lax.axis_index("grp")]).astype(jnp.int32)

    depth = out_w.shape[0]
    ring = depth == width and cores == 2
    cut = width * FIRST // 8 if ring else depth

    def own_half(start, stop):
        half = (stop - start) // cores
        return lax.dynamic_slice_in_dim(out_w, start + core * half, half, axis=0)

    first = lax.all_gather(own_half(0, cut), ("ctx", "dp"), axis=0, tiled=True)
    weights = [Gathered(first, members, 0)]
    if ring:
        near = [around(own_half(cut, depth))]

    x = jnp.transpose(projected, (2, 0, 1, 3))
    filters = medium_h.astype(F32)
    empty = jnp.zeros_like(filters)
    causal = jnp.concatenate([empty[:, :1], filters[:, ::-1], empty[:, 1:]], axis=1)
    anticausal = jnp.concatenate([filters, empty], axis=1)

    cotangent = grad_out.reshape(seqs * rows, width)
    product, pack = products(x, short_w, taps)
    mixed_high, gated_high = mix_high(causal, product, x, short_w, taps, group_size)
    high = [gated_high] + [to(gated_high, k) for k in partners[1:]]
    if ring:
        near.append(around(after(near[-1], mixed_high)))
        for _ in range(length - 3):
            near.append(around(after(near[-1], *high[1:])))

    def send_parts(piece, ready, before):
        parts = grad_parts(pos, after(cotangent, *ready), piece, members)
        shape = (seqs, rows, piece.span)
        parts = [after(block, *before) for block in parts]
        sent = [parts[0]] + [to(parts[k], k) for k in partners[1:]]
        return [block.reshape(shape) for block in sent]

    all_terms = [send_parts(weights[0], high[1:], [])]
    if ring:
        near[-1] = after(near[-1], *all_terms[0][1:3])
        pack = after(pack, near[-1])
        weights.append(Passed(out_w, near, [swap(block) for block in near], cut))
        all_terms.append(send_parts(weights[1], [], all_terms[0][1:]))

    front = shift(pack, "ctx", 1)
    mixed_low, gated_low, head = mix_low(causal, front, product, x, short_w, taps, group_size)
    sent = after(gated_low, all_terms[-1][0])
    low = [gated_low] + [to(sent, k) for k in partners[1:]]
    block_out = block_output(pos, weights, high, 1, 2, None)

    outs, sums = [], []
    for p, piece in enumerate(weights):
        terms = all_terms[p]
        if p:
            terms = [after(terms[0], outs[-1], block_out)] + terms[1:]
        mix_grad, query_grad, pack = mix_grads(
            terms, (mixed_low, mixed_high), x, front, short_w, piece.start
        )
        back = shift(pack, "ctx", -1)
        back = after(back, *([] if p else [block_out]))
        folded = filter_sums(mix_grad, product, head, front, taps, piece.start, group_size)
        grad, part = input_grads(
            anticausal,
            mix_grad,
            query_grad,
            back,
            x,
            front,
            short_w,
            folded,
            piece.start,
            group_size,
        )
        outs.append(grad)
        sums.append(part)
    block_out = block_output(pos, weights, low, 0, 2, block_out)
    total = total_over(jnp.concatenate(sums, axis=0), ("dp", "ctx"))

    grad_projected = jnp.transpose(jnp.concatenate(outs, axis=3), (1, 2, 0, 3))
    filter_total = total[:, :groups].reshape(-1, taps)[:, ::-1]
    short_total = jnp.swapaxes(total[:, groups : groups + 9], 0, 1).reshape(3, 3, width)
    seq_total = seqs * cores
    length_total = rows * length
    filter_grad = filter_total / math.sqrt(seq_total * length_total * group_size)
    short_grad = short_total / math.sqrt(seq_total * length_total)
    return (block_out, grad_projected, filter_grad, short_grad)


def solution(mesh):
    in_specs = (
        P("dp", "ctx", None, "grp"),
        P(None, None, "grp"),
        P("grp", None),
        P("ctx", "grp"),
        P("dp", "ctx", "grp"),
    )
    out_specs = (
        P("dp", "ctx", "grp"),
        P("dp", "ctx", None, "grp"),
        P("grp", None),
        P(None, None, "grp"),
    )
    return jax.shard_map(shards, mesh=mesh, in_specs=in_specs, out_specs=out_specs, check_vma=False)
```

```python
import functools
import math

import jax
import jax.numpy as jnp
from jax import lax
from jax.experimental import pallas as pl
from jax.experimental.pallas import tpu as pltpu
from jax.sharding import PartitionSpec as P

LANES = 128
HALO = 144
FIRST = 3
EXTRA = 16
F32 = jnp.float32
BF16 = jnp.bfloat16


def params(mib=24):
    return pltpu.CompilerParams(vmem_limit_bytes=mib * 1024 * 1024)


def shift(block, axis, distance):
    devices = range(lax.axis_size(axis))
    route = [(i, i + distance) for i in devices if i + distance in devices]
    return lax.ppermute(block, axis, route)


def after(block, *others):
    return lax.optimization_barrier((block, *others))[0]


def pick_groups(stacked, rows, group_size):
    width = stacked.shape[1]
    lane = lax.broadcasted_iota(jnp.int32, (1, width), 1) % LANES
    groups = LANES // group_size
    total = stacked[:rows]
    for g in range(1, groups):
        total = jnp.where(lane >= g * group_size, stacked[g * rows : (g + 1) * rows], total)
    return total


def fill_band(line_ref, band_ref, rows):
    for g in range(line_ref.shape[0]):
        wide = jnp.broadcast_to(line_ref[g : g + 1, :], (rows, line_ref.shape[1]))
        moved = pltpu.roll(wide, 0, 1, stride=1, stride_axis=0)
        band_ref[g * rows : (g + 1) * rows, :] = moved.astype(BF16)


def convolve(x_ref, w_ref, pad, j, s, head):
    rows = x_ref.shape[2]
    own = s * 3 + j
    pad[own, 0:8] = head
    pad[own, 8 : 8 + rows] = x_ref[j, s].astype(F32)
    total = w_ref[j, 0:1] * pad[own, 8 : 8 + rows]
    total = total + w_ref[j, 1:2] * pad[own, 7 : 7 + rows]
    return total + w_ref[j, 2:3] * pad[own, 6 : 6 + rows]


def front_rows(front_ref, j, s, taps):
    return front_ref[s, taps : taps + 2 * EXTRA].astype(F32)[j * 8 : j * 8 + 8]


def product_kernel(x_ref, w_ref, product_ref, pack_ref, pad):
    seqs, rows = x_ref.shape[1], x_ref.shape[2]
    taps = pack_ref.shape[1] - 2 * EXTRA
    nothing = jnp.zeros((8, LANES), F32)
    for s in range(seqs):
        keys = convolve(x_ref, w_ref, pad, 1, s, nothing)
        values = convolve(x_ref, w_ref, pad, 2, s, nothing)
        product = (keys * values).astype(BF16)
        product_ref[s] = product
        pack_ref[s, :taps] = product[rows - taps :]
        tails = [x_ref[j, s, rows - 16 :].astype(F32)[8:] for j in range(3)]
        pack_ref[s, taps:] = jnp.concatenate(tails + [nothing], axis=0).astype(BF16)


def products(x, short_w, taps):
    _, seqs, rows, width = x.shape
    at3 = lambda i: (0, 0, i)
    return pl.pallas_call(
        product_kernel,
        grid=(width // LANES,),
        in_specs=[
            pl.BlockSpec((3, seqs, rows, LANES), lambda i: (0, 0, 0, i)),
            pl.BlockSpec((3, 3, LANES), at3),
        ],
        out_specs=[
            pl.BlockSpec((seqs, rows, LANES), at3),
            pl.BlockSpec((seqs, taps + 2 * EXTRA, LANES), at3),
        ],
        out_shape=[
            jax.ShapeDtypeStruct((seqs, rows, width), BF16),
            jax.ShapeDtypeStruct((seqs, taps + 2 * EXTRA, width), BF16),
        ],
        scratch_shapes=[pltpu.VMEM((3 * seqs, rows + 8, LANES), F32)],
        compiler_params=params(),
        name="products",
    )(x, short_w)


def mix_high_kernel(
    group_size, line_ref, low_ref, high_ref, x_ref, w_ref, mixed_ref, gated_ref, band, columns, pad
):
    seqs, rows = low_ref.shape[0], low_ref.shape[1]
    fill_band(line_ref, band, rows)
    for s in range(seqs):
        at = slice(s * LANES, (s + 1) * LANES)
        columns[:rows, at] = low_ref[s]
        columns[rows:, at] = high_ref[s]
    stacked = jnp.dot(band[...], columns[...], preferred_element_type=F32)
    mixed = pick_groups(stacked, rows, group_size)
    nothing = jnp.zeros((8, LANES), F32)
    for s in range(seqs):
        part = mixed[:, s * LANES : (s + 1) * LANES]
        mixed_ref[s] = part
        query = convolve(x_ref, w_ref, pad, 0, s, nothing)[rows:]
        gated_ref[s] = (query * part).astype(BF16)


def mix_high(line, product, x, short_w, rows, group_size):
    _, seqs, length, width = x.shape
    groups = LANES // group_size
    part = lambda at: pl.BlockSpec((seqs, rows, LANES), lambda i: (0, at, i))
    shape = (seqs, rows, width)
    return pl.pallas_call(
        functools.partial(mix_high_kernel, group_size),
        grid=(width // LANES,),
        in_specs=[
            pl.BlockSpec((groups, 2 * rows), lambda i: (i, 0)),
            part(0),
            part(1),
            pl.BlockSpec((1, seqs, length, LANES), lambda i: (0, 0, 0, i)),
            pl.BlockSpec((3, 3, LANES), lambda i: (0, 0, i)),
        ],
        out_specs=[part(0), part(0)],
        out_shape=[jax.ShapeDtypeStruct(shape, F32), jax.ShapeDtypeStruct(shape, BF16)],
        scratch_shapes=[
            pltpu.VMEM((groups * rows, 2 * rows), BF16),
            pltpu.VMEM((2 * rows, seqs * LANES), BF16),
            pltpu.VMEM((3 * seqs, length + 8, LANES), F32),
        ],
        compiler_params=params(),
        name="mix_high",
    )(line, product, product, x, short_w)


def mix_low_kernel(
    group_size,
    line_ref,
    front_ref,
    product_ref,
    x_ref,
    w_ref,
    mixed_ref,
    gated_ref,
    head_ref,
    band,
    columns,
    pad,
):
    seqs, rows = product_ref.shape[0], product_ref.shape[1]
    fill_band(line_ref, band, rows)
    queries = []
    for s in range(seqs):
        at = slice(s * LANES, (s + 1) * LANES)
        found = [
            convolve(x_ref, w_ref, pad, j, s, front_rows(front_ref, j, s, rows)) for j in range(3)
        ]
        queries.append(found[0])
        head = (found[1][:EXTRA] * found[2][:EXTRA]).astype(BF16)
        head_ref[s] = head
        columns[:rows, at] = front_ref[s, :rows]
        columns[rows : rows + EXTRA, at] = head
        columns[rows + EXTRA :, at] = product_ref[s, EXTRA:]
    stacked = jnp.dot(band[...], columns[...], preferred_element_type=F32)
    mixed = pick_groups(stacked, rows, group_size)
    for s in range(seqs):
        part = mixed[:, s * LANES : (s + 1) * LANES]
        mixed_ref[s] = part
        gated_ref[s] = (queries[s] * part).astype(BF16)


def mix_low(line, front, product, x, short_w, rows, group_size):
    _, seqs, _, width = x.shape
    groups = LANES // group_size
    part = lambda count: pl.BlockSpec((seqs, count, LANES), lambda i: (0, 0, i))
    shape = (seqs, rows, width)
    return pl.pallas_call(
        functools.partial(mix_low_kernel, group_size),
        grid=(width // LANES,),
        in_specs=[
            pl.BlockSpec((groups, 2 * rows), lambda i: (i, 0)),
            part(front.shape[1]),
            part(rows),
            pl.BlockSpec((3, seqs, rows, LANES), lambda i: (0, 0, 0, i)),
            pl.BlockSpec((3, 3, LANES), lambda i: (0, 0, i)),
        ],
        out_specs=[part(rows), part(rows), part(EXTRA)],
        out_shape=[
            jax.ShapeDtypeStruct(shape, F32),
            jax.ShapeDtypeStruct(shape, BF16),
            jax.ShapeDtypeStruct((seqs, EXTRA, width), BF16),
        ],
        scratch_shapes=[
            pltpu.VMEM((groups * rows, 2 * rows), BF16),
            pltpu.VMEM((2 * rows, seqs * LANES), BF16),
            pltpu.VMEM((3 * seqs, rows + 8, LANES), F32),
        ],
        compiler_params=params(),
        name="mix_low",
    )(line, front, product, x, short_w)


class Gathered:
    def __init__(self, w, steps, start):
        self.arrays, self.start, self.span = [w], start, w.shape[0] // steps

    def fetch(self, pos_ref, refs, buffer, base, sems, partner):
        owner = lax.bitwise_xor(pos_ref[2], partner)
        rows = pl.ds(pl.multiple_of(owner * self.span, self.span), self.span)
        place = buffer.at[partner, pl.ds(base, self.span)]
        copy = pltpu.make_async_copy(refs[0].at[rows], place, sems.at[partner, 0])
        copy.start()
        return [copy]


class Passed:
    def __init__(self, own, near, far, start):
        self.arrays, self.start, self.span = [own, *near, *far], start, 2 * near[0].shape[0]

    def fetch(self, pos_ref, refs, buffer, base, sems, partner):
        steps, half = (len(refs) + 1) // 2, self.span // 2
        owner = lax.bitwise_xor(pos_ref[2], partner)
        step = lax.rem(pos_ref[0] - owner + steps, steps)
        mine = pl.multiple_of(pos_ref[1] * half, half)
        other = pl.multiple_of((1 - pos_ref[1]) * half, half)

        def copies(first, second):
            return [
                pltpu.make_async_copy(
                    source, buffer.at[partner, pl.ds(base + place, half)], sems.at[partner, which]
                )
                for which, (source, place) in enumerate(((first, mine), (second, other)))
            ]

        for distance in range(steps):

            @pl.when(step == distance)
            def _(distance=distance):
                if distance == 0:
                    pair = [refs[0].at[pl.ds(self.start + at, half)] for at in (mine, other)]
                else:
                    pair = [refs[distance], refs[steps - 1 + distance]]
                for copy in copies(*pair):
                    copy.start()

        return copies(refs[1], refs[steps])


def grad_kernel(weights, steps, ranges, pos_ref, cot_ref, *refs):
    held = len(weights.arrays)
    outs, (buffer, sems) = refs[held:-2], refs[-2:]
    order = list(range(1, steps)) + [0]
    copies = {
        partner: weights.fetch(pos_ref, refs[:held], buffer, 0, sems, partner)
        for partner in order
    }
    for partner in order:
        for copy in copies[partner]:
            copy.wait()
        part = lax.dot_general(
            cot_ref[...],
            buffer[partner],
            (((1,), (1,)), ((), ())),
            preferred_element_type=F32,
        )
        if partner == 0:
            outs[0][...] = part.reshape(outs[0].shape)
            continue
        for r, (start, stop) in enumerate(ranges):
            out_ref = outs[1 + r * (steps - 1) + partner - 1]
            rows = outs[0].shape[1]
            for s in range(out_ref.shape[0]):
                out_ref[s] = part[s * rows + start : s * rows + stop].astype(BF16)


def grad_parts(pos, cotangent, weights, steps, ranges):
    seqs, rows, width = cotangent.shape
    span = weights.span
    inside = pl.BlockSpec(memory_space=pltpu.VMEM)
    shapes = [jax.ShapeDtypeStruct((seqs, rows, span), F32)]
    for start, stop in ranges:
        shapes += [jax.ShapeDtypeStruct((seqs, stop - start, span), BF16)] * (steps - 1)
    found = pl.pallas_call(
        functools.partial(grad_kernel, weights, steps, ranges),
        in_specs=[pl.BlockSpec(memory_space=pltpu.SMEM), inside]
        + [pl.BlockSpec(memory_space=pltpu.HBM)] * len(weights.arrays),
        out_specs=[inside] * len(shapes),
        out_shape=shapes,
        scratch_shapes=[
            pltpu.VMEM((steps, span, width), BF16),
            pltpu.SemaphoreType.DMA((steps, 2)),
        ],
        compiler_params=params(24),
        name="grad_parts",
    )(pos, cotangent.reshape(seqs * rows, width), *weights.arrays)
    return found[0], [
        found[1 + r * (steps - 1) : 1 + (r + 1) * (steps - 1)] for r in range(len(ranges))
    ]


def out_kernel(weights, steps, pos_ref, *refs):
    out_ref, buffer, *sems = refs[-2 - len(weights) :]
    copies = {partner: [] for partner in range(steps)}
    for piece, piece_sems in zip(weights, sems):
        held, refs = refs[: len(piece.arrays)], refs[len(piece.arrays) :]
        for partner in range(steps):
            copies[partner] += piece.fetch(
                pos_ref, held, buffer, piece.start, piece_sems, partner
            )
    total = None
    for partner in range(steps):
        for copy in copies[partner]:
            copy.wait()
        left = refs[partner][...].reshape(-1, buffer.shape[1])
        term = jnp.dot(left, buffer[partner], preferred_element_type=F32)
        total = term if total is None else total + term
    out_ref[...] = total.astype(BF16).reshape(out_ref.shape)


def block_output(pos, weights, gated, at, blocks, before):
    steps = len(gated)
    seqs, rows, depth = gated[0].shape
    width = weights[0].arrays[0].shape[1]
    inside = pl.BlockSpec(memory_space=pltpu.VMEM)
    anywhere = pl.BlockSpec(memory_space=pltpu.HBM)
    arrays = [array for piece in weights for array in piece.arrays]
    before = [] if before is None else [before]
    return pl.pallas_call(
        functools.partial(out_kernel, weights, steps),
        grid=(1,),
        in_specs=[pl.BlockSpec(memory_space=pltpu.SMEM)]
        + [anywhere] * len(arrays)
        + [inside] * steps
        + [anywhere] * len(before),
        out_specs=pl.BlockSpec((seqs, rows, width), lambda i: (0, at, 0)),
        out_shape=jax.ShapeDtypeStruct((seqs, blocks * rows, width), BF16),
        scratch_shapes=[pltpu.VMEM((steps, depth, width), BF16)]
        + [pltpu.SemaphoreType.DMA((steps, 2))] * len(weights),
        input_output_aliases={1 + len(arrays) + steps: 0} if before else {},
        compiler_params=params(24),
        name="block_output",
    )(pos, *arrays, *gated, *before)


def mix_grad_kernel(count, start, stop, *refs):
    terms = refs[:count]
    low_ref, high_ref, x_ref, front_ref, w_ref, mix_ref, query_ref = refs[count : count + 7]
    pad = refs[-1]
    seqs, half = x_ref.shape[1], low_ref.shape[1]
    for s in range(seqs):
        query = convolve(x_ref, w_ref, pad, 0, s, front_rows(front_ref, 0, s, half))
        for first, mixed_ref in ((0, low_ref), (half, high_ref)):
            begin, end = max(first, start), min(first + half, stop)
            if begin >= end:
                continue
            at = slice(begin - start, end - start)
            total = terms[0][s, begin:end]
            for term in terms[1:]:
                total = total + term[s, at].astype(F32)
            gated_grad = total.astype(BF16).astype(F32)
            mixed = mixed_ref[s, begin - first : end - first]
            mix_ref[s, at] = (gated_grad * query[begin:end]).astype(BF16)
            query_ref[s, at] = (gated_grad * mixed).astype(BF16)
        if start == 0:
            pack_ref = refs[count + 7]
            pack_ref[s, :HALO] = mix_ref[s, :HALO]
            pack_ref[s, HALO : HALO + EXTRA] = query_ref[s, :EXTRA]
            heads = [x_ref[j, s, :EXTRA].astype(F32)[:8] for j in (1, 2)]
            pack_ref[s, HALO + EXTRA :] = jnp.concatenate(heads, axis=0).astype(BF16)


def mix_grads(own, terms, start, stop, mixed, x, front, short_w, offset):
    seqs, rows, width = own.shape
    half = rows // 2
    first = offset // LANES
    local = lambda count: pl.BlockSpec((seqs, count, LANES), lambda i: (0, 0, i))
    wide = lambda count: pl.BlockSpec((seqs, count, LANES), lambda i: (0, 0, first + i))
    counts = [stop - start] * 2 + [HALO + 2 * EXTRA] * (start == 0)
    return pl.pallas_call(
        functools.partial(mix_grad_kernel, 1 + len(terms), start, stop),
        grid=(width // LANES,),
        in_specs=[local(rows)]
        + [local(stop - start)] * len(terms)
        + [wide(half), wide(half)]
        + [
            pl.BlockSpec((3, seqs, rows, LANES), lambda i: (0, 0, 0, first + i)),
            wide(front.shape[1]),
            pl.BlockSpec((3, 3, LANES), lambda i: (0, 0, first + i)),
        ],
        out_specs=[local(count) for count in counts],
        out_shape=[jax.ShapeDtypeStruct((seqs, count, width), BF16) for count in counts],
        scratch_shapes=[pltpu.VMEM((3 * seqs, rows + 8, LANES), F32)],
        compiler_params=params(),
        name="mix_grads",
    )(own, *terms, *mixed, x, front, short_w)


def join(parts, whole_ref):
    at = 0
    for part_ref in parts:
        whole_ref[:, at : at + part_ref.shape[1]] = part_ref[...]
        at += part_ref.shape[1]


def filter_kernel(group_size, ranges, *refs):
    product_ref, head_ref, front_ref, out_ref, left, columns, mix_ref = refs[ranges:]
    join(refs[:ranges], mix_ref)
    seqs = mix_ref.shape[0]
    rows = out_ref.shape[1]
    groups = LANES // group_size
    lane = lax.broadcasted_iota(jnp.int32, (1, LANES), 1) // group_size
    total = None
    for b in range(mix_ref.shape[1] // rows):
        for s in range(seqs):
            at = slice(s * LANES, (s + 1) * LANES)
            block = mix_ref[s, b * rows : (b + 1) * rows]
            for g in range(groups):
                keep = (lane == g).astype(F32).astype(BF16)
                left[b, g * rows : (g + 1) * rows, at] = block * keep
            if b == 0:
                columns[b, :rows, at] = front_ref[s, :rows]
            else:
                columns[b, :rows, at] = product_ref[s, (b - 1) * rows : b * rows]
            columns[b, rows:, at] = product_ref[s, b * rows : (b + 1) * rows]
            if b < 2:
                start = (1 - b) * rows
                columns[b, start : start + EXTRA, at] = head_ref[s]
        term = lax.dot_general(
            left[b], columns[b], (((1,), (1,)), ((), ())), preferred_element_type=F32
        )
        total = term if total is None else total + term
    span = 2 * rows
    folded = []
    for g in range(groups):
        sum_g = None
        for a in range(rows // 8):
            tile = total[g * rows + a * 8 : g * rows + a * 8 + 8]
            tile = pltpu.roll(tile, (span - a * 8) % span, 1)
            sum_g = tile if sum_g is None else sum_g + tile
        folded.append(sum_g)
    stacked = jnp.stack(folded, axis=0)
    result = None
    for r in range(8):
        row = pltpu.roll(stacked[:, r, :], span - r - 1, 1)
        result = row if result is None else result + row
    out_ref[...] = result[:, :rows]


def filter_sums(mix_grad, product, head, front, block_rows, offset, group_size):
    seqs, rows, _ = product.shape
    width = mix_grad[0].shape[2]
    first = offset // LANES
    groups = LANES // group_size
    blocks = rows // block_rows
    return pl.pallas_call(
        functools.partial(filter_kernel, group_size, len(mix_grad)),
        grid=(width // LANES,),
        in_specs=[
            pl.BlockSpec((seqs, part.shape[1], LANES), lambda i: (0, 0, i)) for part in mix_grad
        ]
        + [
            pl.BlockSpec((seqs, rows, LANES), lambda i: (0, 0, first + i)),
            pl.BlockSpec((seqs, EXTRA, LANES), lambda i: (0, 0, first + i)),
            pl.BlockSpec((seqs, front.shape[1], LANES), lambda i: (0, 0, first + i)),
        ],
        out_specs=pl.BlockSpec((groups, block_rows), lambda i: (i, 0)),
        out_shape=jax.ShapeDtypeStruct((width // group_size, block_rows), F32),
        scratch_shapes=[
            pltpu.VMEM((blocks, groups * block_rows, seqs * LANES), BF16),
            pltpu.VMEM((blocks, 2 * block_rows, seqs * LANES), BF16),
            pltpu.VMEM((seqs, rows, LANES), BF16),
        ],
        compiler_params=params(),
        name="filter_sums",
    )(*mix_grad, product, head, front)


def input_grad_kernel(group_size, ranges, *refs):
    line_ref, back_ref, x_ref, front_ref, w_ref, filter_ref = refs[2 * ranges : 2 * ranges + 6]
    out_ref, sums_ref, band, columns, grads, inputs, edge, mix_ref, query_ref = refs[2 * ranges + 6 :]
    join(refs[:ranges], mix_ref)
    join(refs[ranges : 2 * ranges], query_ref)
    seqs, rows = mix_ref.shape[0], mix_ref.shape[1]
    block = line_ref.shape[1] // 2
    groups = LANES // group_size
    fill_band(line_ref, band, block)
    found = []
    for b in range(rows // block):
        for s in range(seqs):
            at = slice(s * LANES, (s + 1) * LANES)
            columns[b, :block, at] = mix_ref[s, b * block : (b + 1) * block]
            if (b + 1) * block < rows:
                columns[b, block:, at] = mix_ref[s, (b + 1) * block : (b + 2) * block]
            else:
                columns[b, block:, at] = back_ref[s, :block]
        stacked = jnp.dot(band[...], columns[b], preferred_element_type=F32)
        found.append(pick_groups(stacked, block, group_size))
    last = rows // block
    for s in range(seqs):
        at = slice(s * LANES, (s + 1) * LANES)
        columns[last, :HALO, at] = back_ref[s, :HALO]
        columns[last, HALO:, at] = jnp.zeros((2 * block - HALO, LANES), BF16)
    few = jnp.concatenate([band[g * block : g * block + EXTRA] for g in range(groups)], axis=0)
    stacked = jnp.dot(few, columns[last], preferred_element_type=F32)
    beyond = pick_groups(stacked, EXTRA, group_size)
    for s in range(seqs):
        at = slice(s * LANES, (s + 1) * LANES)
        after = []
        for j in (1, 2):
            own = s * 2 + j - 1
            edge[own, 0:8] = x_ref[j, s, rows - 16 :].astype(F32)[8:]
            edge[own, 8:16] = back_ref[s, HALO + EXTRA :].astype(F32)[8 * j - 8 : 8 * j]
            total = w_ref[j, 0:1] * edge[own, 8:16]
            total = total + w_ref[j, 1:2] * edge[own, 7:15]
            total = total + w_ref[j, 2:3] * edge[own, 6:14]
            after.append(total)
        streams = [
            convolve(x_ref, w_ref, inputs, j, s, front_rows(front_ref, j, s, block))
            for j in range(1, 3)
        ]
        inputs[s * 3, 0:8] = front_rows(front_ref, 0, s, block)
        inputs[s * 3, 8 : 8 + rows] = x_ref[0, s].astype(F32)
        for j in range(3):
            own = s * 3 + j
            if j == 0:
                grads[own, :rows] = query_ref[s].astype(F32)
                grads[own, rows:] = back_ref[s, HALO : HALO + EXTRA].astype(F32)[:8]
            else:
                factor = streams[2 - j]
                for b in range(rows // block):
                    part = slice(b * block, (b + 1) * block)
                    value = found[b][:, at] * factor[part]
                    grads[own, part] = value.astype(BF16).astype(F32)
                value = beyond[:8, at] * after[2 - j]
                grads[own, rows:] = value.astype(BF16).astype(F32)
            total = None
            for i in range(3):
                term = w_ref[j, i : i + 1] * grads[own, i : i + rows]
                total = term if total is None else total + term
            out_ref[j, s] = total.astype(BF16)
    for j in range(3):
        for i in range(3):
            total = None
            for s in range(seqs):
                own = s * 3 + j
                term = grads[own, :rows] * inputs[own, 8 - i : 8 - i + rows]
                term = jnp.sum(term, axis=0, keepdims=True)
                total = term if total is None else total + term
            sums_ref[0, groups + j * 3 + i : groups + j * 3 + i + 1] = total
    sums_ref[0, :groups] = filter_ref[...]
    sums_ref[0, groups + 9 :] = jnp.zeros((sums_ref.shape[1] - groups - 9, LANES), F32)


def input_grads(
    line, mix_grad, query_grad, back, x, front, short_w, filter_part, offset, group_size
):
    _, seqs, rows, _ = x.shape
    width = back.shape[2]
    block = line.shape[1] // 2
    first = offset // LANES
    groups = LANES // group_size
    local = lambda count: pl.BlockSpec((seqs, count, LANES), lambda i: (0, 0, i))
    wide3 = lambda *sizes: pl.BlockSpec(sizes + (LANES,), lambda i: (0, 0, first + i))
    wide4 = lambda *sizes: pl.BlockSpec(sizes + (LANES,), lambda i: (0, 0, 0, first + i))
    return pl.pallas_call(
        functools.partial(input_grad_kernel, group_size, len(mix_grad)),
        grid=(width // LANES,),
        in_specs=[local(part.shape[1]) for part in (*mix_grad, *query_grad)]
        + [
            pl.BlockSpec((groups, 2 * block), lambda i: (first + i, 0)),
            local(HALO + 2 * EXTRA),
            wide4(3, seqs, rows),
            wide3(seqs, front.shape[1]),
            wide3(3, 3),
            pl.BlockSpec((groups, block), lambda i: (i, 0)),
        ],
        out_specs=[
            pl.BlockSpec((3, seqs, rows, LANES), lambda i: (0, 0, 0, i)),
            pl.BlockSpec((1, groups + 16, LANES), lambda i: (i, 0, 0)),
        ],
        out_shape=[
            jax.ShapeDtypeStruct((3, seqs, rows, width), BF16),
            jax.ShapeDtypeStruct((width // LANES, groups + 16, LANES), F32),
        ],
        scratch_shapes=[
            pltpu.VMEM((groups * block, 2 * block), BF16),
            pltpu.VMEM((rows // block + 1, 2 * block, seqs * LANES), BF16),
            pltpu.VMEM((3 * seqs, rows + 8, LANES), F32),
            pltpu.VMEM((3 * seqs, rows + 8, LANES), F32),
            pltpu.VMEM((2 * seqs, 16, LANES), F32),
            pltpu.VMEM((seqs, rows, LANES), BF16),
            pltpu.VMEM((seqs, rows, LANES), BF16),
        ],
        compiler_params=params(),
        name="input_grads",
    )(*mix_grad, *query_grad, line, back, x, front, short_w, filter_part)


def total_over(block, axes):
    count = math.prod(lax.axis_size(axis) for axis in axes)
    if count & (count - 1):
        return lax.psum(block, axes)
    step = count // 2
    order = []
    while step:
        order.append(step)
        step //= 2
    for step in order:
        block = block + lax.ppermute(block, axes, [(i, i ^ step) for i in range(count)])
    return block


def shards(projected, short_w, medium_h, out_w, grad_out):
    seqs, rows, _, width = projected.shape
    taps = medium_h.shape[1]
    group_size = width // medium_h.shape[0]
    groups = LANES // group_size
    members = lax.axis_size("grp")
    cores = lax.axis_size("dp")
    length = lax.axis_size("ctx")
    partners = range(members)
    to = lambda block, k: lax.ppermute(block, "grp", [(i, i ^ k) for i in partners])
    around = lambda block: lax.ppermute(block, "ctx", [(i, (i + 1) % length) for i in range(length)])
    swap = lambda block: lax.ppermute(block, "dp", [(0, 1), (1, 0)])
    core = lax.axis_index("dp")
    pos = jnp.stack([lax.axis_index("ctx"), core, lax.axis_index("grp")]).astype(jnp.int32)

    depth = out_w.shape[0]
    ring = depth == width and cores == 2
    cut = width * FIRST // 8 if ring else depth

    def own_half(start, stop):
        half = (stop - start) // cores
        return lax.dynamic_slice_in_dim(out_w, start + core * half, half, axis=0)

    first = lax.all_gather(own_half(0, cut), ("ctx", "dp"), axis=0, tiled=True)
    weights = [Gathered(first, members, 0)]
    if ring:
        near = [around(own_half(cut, depth))]

    x = jnp.transpose(projected, (2, 0, 1, 3))
    filters = medium_h.astype(F32)
    empty = jnp.zeros_like(filters)
    causal = jnp.concatenate([empty[:, :1], filters[:, ::-1], empty[:, 1:]], axis=1)
    anticausal = jnp.concatenate([filters, empty], axis=1)

    product, pack = products(x, short_w, taps)
    mixed_high, gated_high = mix_high(causal, product, x, short_w, taps, group_size)
    high = [gated_high] + [to(gated_high, k) for k in partners[1:]]
    if ring:
        near.append(around(after(near[-1], mixed_high)))
        for _ in range(length - 3):
            near.append(around(after(near[-1], *high[1:])))

    def send_parts(piece, ranges, ready, before):
        own, parts = grad_parts(pos, after(grad_out, *ready), piece, members, ranges)
        sent = [[after(block, *before) for block in blocks] for blocks in parts]
        return own, [[to(block, k + 1) for k, block in enumerate(blocks)] for blocks in sent]

    ranges = [[(0, rows)]]
    own, got = send_parts(weights[0], ranges[0], high[1:], [])
    owns, gots = [own], [got]
    if ring:
        near[-1] = after(near[-1], *got[0][:2])
        weights.append(Passed(out_w, near, [swap(block) for block in near], cut))
        ranges.append([(0, rows)])
        own, got = send_parts(weights[1], ranges[1], [], got[0])
        owns.append(own)
        gots.append(got)

    block_out = block_output(pos, weights, high, 1, 2, None)
    front = shift(after(pack, owns[-1]), "ctx", 1)
    front = after(front, block_out)
    mixed_low, gated_low, head = mix_low(causal, front, product, x, short_w, taps, group_size)
    sent = after(gated_low, owns[-1])
    low = [gated_low] + [to(sent, k) for k in partners[1:]]

    outs, sums = [], []
    for p, piece in enumerate(weights):
        mix_grad, query_grad, back = [], [], None
        for (start, stop), terms in zip(ranges[p], gots[p]):
            held = after(owns[p], outs[-1], block_out) if p else owns[p]
            found = mix_grads(
                held,
                terms,
                start,
                stop,
                (mixed_low, mixed_high),
                x,
                front,
                short_w,
                piece.start,
            )
            mix_grad.append(found[0])
            query_grad.append(found[1])
            if start == 0:
                back = shift(found[2], "ctx", -1)
        back = after(back, *([] if p else [block_out]))
        folded = filter_sums(mix_grad, product, head, front, taps, piece.start, group_size)
        grad, part = input_grads(
            anticausal,
            mix_grad,
            query_grad,
            back,
            x,
            front,
            short_w,
            folded,
            piece.start,
            group_size,
        )
        outs.append(grad)
        sums.append(part)
    block_out = block_output(pos, weights, low, 0, 2, block_out)
    total = total_over(jnp.concatenate(sums, axis=0), ("dp", "ctx"))

    grad_projected = jnp.transpose(jnp.concatenate(outs, axis=3), (1, 2, 0, 3))
    filter_total = total[:, :groups].reshape(-1, taps)[:, ::-1]
    short_total = jnp.swapaxes(total[:, groups : groups + 9], 0, 1).reshape(3, 3, width)
    seq_total = seqs * cores
    length_total = rows * length
    filter_grad = filter_total / math.sqrt(seq_total * length_total * group_size)
    short_grad = short_total / math.sqrt(seq_total * length_total)
    return (block_out, grad_projected, filter_grad, short_grad)


def solution(mesh):
    in_specs = (
        P("dp", "ctx", None, "grp"),
        P(None, None, "grp"),
        P("grp", None),
        P("ctx", "grp"),
        P("dp", "ctx", "grp"),
    )
    out_specs = (
        P("dp", "ctx", "grp"),
        P("dp", "ctx", None, "grp"),
        P("grp", None),
        P(None, None, "grp"),
    )
    return jax.shard_map(shards, mesh=mesh, in_specs=in_specs, out_specs=out_specs, check_vma=False)
```

```python
import functools
import math

import jax
import jax.numpy as jnp
from jax import lax
from jax.experimental import pallas as pl
from jax.experimental.pallas import tpu as pltpu
from jax.sharding import PartitionSpec as P

LANES = 128
HALO = 144
FIRST = 3
EXTRA = 16
F32 = jnp.float32
BF16 = jnp.bfloat16


def params(mib=24):
    return pltpu.CompilerParams(vmem_limit_bytes=mib * 1024 * 1024)


def shift(block, axis, distance):
    devices = range(lax.axis_size(axis))
    route = [(i, i + distance) for i in devices if i + distance in devices]
    return lax.ppermute(block, axis, route)


def after(block, *others):
    return lax.optimization_barrier((block, *others))[0]


def pick_groups(stacked, rows, group_size):
    width = stacked.shape[1]
    lane = lax.broadcasted_iota(jnp.int32, (1, width), 1) % LANES
    groups = LANES // group_size
    total = stacked[:rows]
    for g in range(1, groups):
        total = jnp.where(lane >= g * group_size, stacked[g * rows : (g + 1) * rows], total)
    return total


def fill_band(line_ref, band_ref, rows):
    for g in range(line_ref.shape[0]):
        wide = jnp.broadcast_to(line_ref[g : g + 1, :], (rows, line_ref.shape[1]))
        moved = pltpu.roll(wide, 0, 1, stride=1, stride_axis=0)
        band_ref[g * rows : (g + 1) * rows, :] = moved.astype(BF16)


def convolve(x_ref, w_ref, pad, j, s, head):
    rows = x_ref.shape[2]
    own = s * 3 + j
    pad[own, 0:8] = head
    pad[own, 8 : 8 + rows] = x_ref[j, s].astype(F32)
    total = w_ref[j, 0:1] * pad[own, 8 : 8 + rows]
    total = total + w_ref[j, 1:2] * pad[own, 7 : 7 + rows]
    return total + w_ref[j, 2:3] * pad[own, 6 : 6 + rows]


def front_rows(front_ref, j, s, taps):
    return front_ref[s, taps : taps + 2 * EXTRA].astype(F32)[j * 8 : j * 8 + 8]


def product_kernel(x_ref, w_ref, product_ref, pack_ref, pad):
    seqs, rows = x_ref.shape[1], x_ref.shape[2]
    taps = pack_ref.shape[1] - 2 * EXTRA
    nothing = jnp.zeros((8, LANES), F32)
    for s in range(seqs):
        keys = convolve(x_ref, w_ref, pad, 1, s, nothing)
        values = convolve(x_ref, w_ref, pad, 2, s, nothing)
        product = (keys * values).astype(BF16)
        product_ref[s] = product
        pack_ref[s, :taps] = product[rows - taps :]
        tails = [x_ref[j, s, rows - 16 :].astype(F32)[8:] for j in range(3)]
        pack_ref[s, taps:] = jnp.concatenate(tails + [nothing], axis=0).astype(BF16)


def products(x, short_w, taps):
    _, seqs, rows, width = x.shape
    at3 = lambda i: (0, 0, i)
    return pl.pallas_call(
        product_kernel,
        grid=(width // LANES,),
        in_specs=[
            pl.BlockSpec((3, seqs, rows, LANES), lambda i: (0, 0, 0, i)),
            pl.BlockSpec((3, 3, LANES), at3),
        ],
        out_specs=[
            pl.BlockSpec((seqs, rows, LANES), at3),
            pl.BlockSpec((seqs, taps + 2 * EXTRA, LANES), at3),
        ],
        out_shape=[
            jax.ShapeDtypeStruct((seqs, rows, width), BF16),
            jax.ShapeDtypeStruct((seqs, taps + 2 * EXTRA, width), BF16),
        ],
        scratch_shapes=[pltpu.VMEM((3 * seqs, rows + 8, LANES), F32)],
        compiler_params=params(),
        name="products",
    )(x, short_w)


def mix_high_kernel(
    group_size, line_ref, low_ref, high_ref, x_ref, w_ref, mixed_ref, gated_ref, band, columns, pad
):
    seqs, rows = low_ref.shape[0], low_ref.shape[1]
    fill_band(line_ref, band, rows)
    for s in range(seqs):
        at = slice(s * LANES, (s + 1) * LANES)
        columns[:rows, at] = low_ref[s]
        columns[rows:, at] = high_ref[s]
    stacked = jnp.dot(band[...], columns[...], preferred_element_type=F32)
    mixed = pick_groups(stacked, rows, group_size)
    nothing = jnp.zeros((8, LANES), F32)
    for s in range(seqs):
        part = mixed[:, s * LANES : (s + 1) * LANES]
        mixed_ref[s] = part
        query = convolve(x_ref, w_ref, pad, 0, s, nothing)[rows:]
        gated_ref[s] = (query * part).astype(BF16)


def mix_high(line, product, x, short_w, rows, group_size):
    _, seqs, length, width = x.shape
    groups = LANES // group_size
    part = lambda at: pl.BlockSpec((seqs, rows, LANES), lambda i: (0, at, i))
    shape = (seqs, rows, width)
    return pl.pallas_call(
        functools.partial(mix_high_kernel, group_size),
        grid=(width // LANES,),
        in_specs=[
            pl.BlockSpec((groups, 2 * rows), lambda i: (i, 0)),
            part(0),
            part(1),
            pl.BlockSpec((1, seqs, length, LANES), lambda i: (0, 0, 0, i)),
            pl.BlockSpec((3, 3, LANES), lambda i: (0, 0, i)),
        ],
        out_specs=[part(0), part(0)],
        out_shape=[jax.ShapeDtypeStruct(shape, F32), jax.ShapeDtypeStruct(shape, BF16)],
        scratch_shapes=[
            pltpu.VMEM((groups * rows, 2 * rows), BF16),
            pltpu.VMEM((2 * rows, seqs * LANES), BF16),
            pltpu.VMEM((3 * seqs, length + 8, LANES), F32),
        ],
        compiler_params=params(),
        name="mix_high",
    )(line, product, product, x, short_w)


def mix_low_kernel(
    group_size,
    line_ref,
    front_ref,
    product_ref,
    x_ref,
    w_ref,
    mixed_ref,
    gated_ref,
    head_ref,
    band,
    columns,
    pad,
):
    seqs, rows = product_ref.shape[0], product_ref.shape[1]
    fill_band(line_ref, band, rows)
    queries = []
    for s in range(seqs):
        at = slice(s * LANES, (s + 1) * LANES)
        found = [
            convolve(x_ref, w_ref, pad, j, s, front_rows(front_ref, j, s, rows)) for j in range(3)
        ]
        queries.append(found[0])
        head = (found[1][:EXTRA] * found[2][:EXTRA]).astype(BF16)
        head_ref[s] = head
        columns[:rows, at] = front_ref[s, :rows]
        columns[rows : rows + EXTRA, at] = head
        columns[rows + EXTRA :, at] = product_ref[s, EXTRA:]
    stacked = jnp.dot(band[...], columns[...], preferred_element_type=F32)
    mixed = pick_groups(stacked, rows, group_size)
    for s in range(seqs):
        part = mixed[:, s * LANES : (s + 1) * LANES]
        mixed_ref[s] = part
        gated_ref[s] = (queries[s] * part).astype(BF16)


def mix_low(line, front, product, x, short_w, rows, group_size):
    _, seqs, _, width = x.shape
    groups = LANES // group_size
    part = lambda count: pl.BlockSpec((seqs, count, LANES), lambda i: (0, 0, i))
    shape = (seqs, rows, width)
    return pl.pallas_call(
        functools.partial(mix_low_kernel, group_size),
        grid=(width // LANES,),
        in_specs=[
            pl.BlockSpec((groups, 2 * rows), lambda i: (i, 0)),
            part(front.shape[1]),
            part(rows),
            pl.BlockSpec((3, seqs, rows, LANES), lambda i: (0, 0, 0, i)),
            pl.BlockSpec((3, 3, LANES), lambda i: (0, 0, i)),
        ],
        out_specs=[part(rows), part(rows), part(EXTRA)],
        out_shape=[
            jax.ShapeDtypeStruct(shape, F32),
            jax.ShapeDtypeStruct(shape, BF16),
            jax.ShapeDtypeStruct((seqs, EXTRA, width), BF16),
        ],
        scratch_shapes=[
            pltpu.VMEM((groups * rows, 2 * rows), BF16),
            pltpu.VMEM((2 * rows, seqs * LANES), BF16),
            pltpu.VMEM((3 * seqs, rows + 8, LANES), F32),
        ],
        compiler_params=params(),
        name="mix_low",
    )(line, front, product, x, short_w)


class Gathered:
    def __init__(self, w, steps, start):
        self.arrays, self.start, self.span = [w], start, w.shape[0] // steps

    def fetch(self, pos_ref, refs, buffer, base, sems, partner):
        owner = lax.bitwise_xor(pos_ref[2], partner)
        rows = pl.ds(pl.multiple_of(owner * self.span, self.span), self.span)
        place = buffer.at[partner, pl.ds(base, self.span)]
        copy = pltpu.make_async_copy(refs[0].at[rows], place, sems.at[partner, 0])
        copy.start()
        return [copy]


class Passed:
    def __init__(self, own, near, far, start):
        self.arrays, self.start, self.span = [own, *near, *far], start, 2 * near[0].shape[0]

    def fetch(self, pos_ref, refs, buffer, base, sems, partner):
        steps, half = (len(refs) + 1) // 2, self.span // 2
        owner = lax.bitwise_xor(pos_ref[2], partner)
        step = lax.rem(pos_ref[0] - owner + steps, steps)
        mine = pl.multiple_of(pos_ref[1] * half, half)
        other = pl.multiple_of((1 - pos_ref[1]) * half, half)

        def copies(first, second):
            return [
                pltpu.make_async_copy(
                    source, buffer.at[partner, pl.ds(base + place, half)], sems.at[partner, which]
                )
                for which, (source, place) in enumerate(((first, mine), (second, other)))
            ]

        for distance in range(steps):

            @pl.when(step == distance)
            def _(distance=distance):
                if distance == 0:
                    pair = [refs[0].at[pl.ds(self.start + at, half)] for at in (mine, other)]
                else:
                    pair = [refs[distance], refs[steps - 1 + distance]]
                for copy in copies(*pair):
                    copy.start()

        return copies(refs[1], refs[steps])


def grad_kernel(weights, steps, ranges, pos_ref, cot_ref, *refs):
    held = len(weights.arrays)
    outs, (buffer, sems) = refs[held:-2], refs[-2:]
    order = list(range(1, steps)) + [0]
    copies = {
        partner: weights.fetch(pos_ref, refs[:held], buffer, 0, sems, partner)
        for partner in order
    }
    for partner in order:
        for copy in copies[partner]:
            copy.wait()
        part = lax.dot_general(
            cot_ref[...],
            buffer[partner],
            (((1,), (1,)), ((), ())),
            preferred_element_type=F32,
        )
        if partner == 0:
            outs[0][...] = part.reshape(outs[0].shape)
            continue
        for r, (start, stop) in enumerate(ranges):
            out_ref = outs[1 + r * (steps - 1) + partner - 1]
            rows = outs[0].shape[1]
            for s in range(out_ref.shape[0]):
                out_ref[s] = part[s * rows + start : s * rows + stop].astype(BF16)


def grad_parts(pos, cotangent, weights, steps, ranges):
    seqs, rows, width = cotangent.shape
    span = weights.span
    inside = pl.BlockSpec(memory_space=pltpu.VMEM)
    shapes = [jax.ShapeDtypeStruct((seqs, rows, span), F32)]
    for start, stop in ranges:
        shapes += [jax.ShapeDtypeStruct((seqs, stop - start, span), BF16)] * (steps - 1)
    found = pl.pallas_call(
        functools.partial(grad_kernel, weights, steps, ranges),
        in_specs=[pl.BlockSpec(memory_space=pltpu.SMEM), inside]
        + [pl.BlockSpec(memory_space=pltpu.HBM)] * len(weights.arrays),
        out_specs=[inside] * len(shapes),
        out_shape=shapes,
        scratch_shapes=[
            pltpu.VMEM((steps, span, width), BF16),
            pltpu.SemaphoreType.DMA((steps, 2)),
        ],
        compiler_params=params(24),
        name="grad_parts",
    )(pos, cotangent.reshape(seqs * rows, width), *weights.arrays)
    return found[0], [
        found[1 + r * (steps - 1) : 1 + (r + 1) * (steps - 1)] for r in range(len(ranges))
    ]


def out_kernel(weights, steps, pos_ref, *refs):
    out_ref, buffer, *sems = refs[-2 - len(weights) :]
    copies = {partner: [] for partner in range(steps)}
    for piece, piece_sems in zip(weights, sems):
        held, refs = refs[: len(piece.arrays)], refs[len(piece.arrays) :]
        for partner in range(steps):
            copies[partner] += piece.fetch(
                pos_ref, held, buffer, piece.start, piece_sems, partner
            )
    total = None
    for partner in range(steps):
        for copy in copies[partner]:
            copy.wait()
        left = refs[partner][...].reshape(-1, buffer.shape[1])
        term = jnp.dot(left, buffer[partner], preferred_element_type=F32)
        total = term if total is None else total + term
    out_ref[...] = total.astype(BF16).reshape(out_ref.shape)


def block_output(pos, weights, gated, at, blocks, before):
    steps = len(gated)
    seqs, rows, depth = gated[0].shape
    width = weights[0].arrays[0].shape[1]
    inside = pl.BlockSpec(memory_space=pltpu.VMEM)
    anywhere = pl.BlockSpec(memory_space=pltpu.HBM)
    arrays = [array for piece in weights for array in piece.arrays]
    before = [] if before is None else [before]
    return pl.pallas_call(
        functools.partial(out_kernel, weights, steps),
        grid=(1,),
        in_specs=[pl.BlockSpec(memory_space=pltpu.SMEM)]
        + [anywhere] * len(arrays)
        + [inside] * steps
        + [anywhere] * len(before),
        out_specs=pl.BlockSpec((seqs, rows, width), lambda i: (0, at, 0)),
        out_shape=jax.ShapeDtypeStruct((seqs, blocks * rows, width), BF16),
        scratch_shapes=[pltpu.VMEM((steps, depth, width), BF16)]
        + [pltpu.SemaphoreType.DMA((steps, 2))] * len(weights),
        input_output_aliases={1 + len(arrays) + steps: 0} if before else {},
        compiler_params=params(24),
        name="block_output",
    )(pos, *arrays, *gated, *before)


def mix_grad_kernel(count, start, stop, *refs):
    terms = refs[:count]
    low_ref, high_ref, x_ref, front_ref, w_ref, mix_ref, query_ref = refs[count : count + 7]
    pad = refs[-1]
    seqs, half = x_ref.shape[1], low_ref.shape[1]
    for s in range(seqs):
        query = convolve(x_ref, w_ref, pad, 0, s, front_rows(front_ref, 0, s, half))
        for first, mixed_ref in ((0, low_ref), (half, high_ref)):
            begin, end = max(first, start), min(first + half, stop)
            if begin >= end:
                continue
            at = slice(begin - start, end - start)
            total = terms[0][s, begin:end]
            for term in terms[1:]:
                total = total + term[s, at].astype(F32)
            gated_grad = total.astype(BF16).astype(F32)
            mixed = mixed_ref[s, begin - first : end - first]
            mix_ref[s, at] = (gated_grad * query[begin:end]).astype(BF16)
            query_ref[s, at] = (gated_grad * mixed).astype(BF16)
        if start == 0:
            pack_ref = refs[count + 7]
            pack_ref[s, :HALO] = mix_ref[s, :HALO]
            pack_ref[s, HALO : HALO + EXTRA] = query_ref[s, :EXTRA]
            heads = [x_ref[j, s, :EXTRA].astype(F32)[:8] for j in (1, 2)]
            pack_ref[s, HALO + EXTRA :] = jnp.concatenate(heads, axis=0).astype(BF16)


def mix_grads(own, terms, start, stop, mixed, x, front, short_w, offset):
    seqs, rows, width = own.shape
    half = rows // 2
    first = offset // LANES
    local = lambda count: pl.BlockSpec((seqs, count, LANES), lambda i: (0, 0, i))
    wide = lambda count: pl.BlockSpec((seqs, count, LANES), lambda i: (0, 0, first + i))
    counts = [stop - start] * 2 + [HALO + 2 * EXTRA] * (start == 0)
    return pl.pallas_call(
        functools.partial(mix_grad_kernel, 1 + len(terms), start, stop),
        grid=(width // LANES,),
        in_specs=[local(rows)]
        + [local(stop - start)] * len(terms)
        + [wide(half), wide(half)]
        + [
            pl.BlockSpec((3, seqs, rows, LANES), lambda i: (0, 0, 0, first + i)),
            wide(front.shape[1]),
            pl.BlockSpec((3, 3, LANES), lambda i: (0, 0, first + i)),
        ],
        out_specs=[local(count) for count in counts],
        out_shape=[jax.ShapeDtypeStruct((seqs, count, width), BF16) for count in counts],
        scratch_shapes=[pltpu.VMEM((3 * seqs, rows + 8, LANES), F32)],
        compiler_params=params(),
        name="mix_grads",
    )(own, *terms, *mixed, x, front, short_w)


def join(parts, whole_ref):
    at = 0
    for part_ref in parts:
        whole_ref[:, at : at + part_ref.shape[1]] = part_ref[...]
        at += part_ref.shape[1]


def filter_kernel(group_size, ranges, *refs):
    product_ref, head_ref, front_ref, out_ref, left, columns, mix_ref = refs[ranges:]
    join(refs[:ranges], mix_ref)
    seqs = mix_ref.shape[0]
    rows = out_ref.shape[1]
    groups = LANES // group_size
    lane = lax.broadcasted_iota(jnp.int32, (1, LANES), 1) // group_size
    total = None
    for b in range(mix_ref.shape[1] // rows):
        for s in range(seqs):
            at = slice(s * LANES, (s + 1) * LANES)
            block = mix_ref[s, b * rows : (b + 1) * rows]
            for g in range(groups):
                keep = (lane == g).astype(F32).astype(BF16)
                left[b, g * rows : (g + 1) * rows, at] = block * keep
            if b == 0:
                columns[b, :rows, at] = front_ref[s, :rows]
            else:
                columns[b, :rows, at] = product_ref[s, (b - 1) * rows : b * rows]
            columns[b, rows:, at] = product_ref[s, b * rows : (b + 1) * rows]
            if b < 2:
                start = (1 - b) * rows
                columns[b, start : start + EXTRA, at] = head_ref[s]
        term = lax.dot_general(
            left[b], columns[b], (((1,), (1,)), ((), ())), preferred_element_type=F32
        )
        total = term if total is None else total + term
    span = 2 * rows
    folded = []
    for g in range(groups):
        sum_g = None
        for a in range(rows // 8):
            tile = total[g * rows + a * 8 : g * rows + a * 8 + 8]
            tile = pltpu.roll(tile, (span - a * 8) % span, 1)
            sum_g = tile if sum_g is None else sum_g + tile
        folded.append(sum_g)
    stacked = jnp.stack(folded, axis=0)
    result = None
    for r in range(8):
        row = pltpu.roll(stacked[:, r, :], span - r - 1, 1)
        result = row if result is None else result + row
    out_ref[...] = result[:, :rows]


def filter_sums(mix_grad, product, head, front, block_rows, offset, group_size):
    seqs, rows, _ = product.shape
    width = mix_grad[0].shape[2]
    first = offset // LANES
    groups = LANES // group_size
    blocks = rows // block_rows
    return pl.pallas_call(
        functools.partial(filter_kernel, group_size, len(mix_grad)),
        grid=(width // LANES,),
        in_specs=[
            pl.BlockSpec((seqs, part.shape[1], LANES), lambda i: (0, 0, i)) for part in mix_grad
        ]
        + [
            pl.BlockSpec((seqs, rows, LANES), lambda i: (0, 0, first + i)),
            pl.BlockSpec((seqs, EXTRA, LANES), lambda i: (0, 0, first + i)),
            pl.BlockSpec((seqs, front.shape[1], LANES), lambda i: (0, 0, first + i)),
        ],
        out_specs=pl.BlockSpec((groups, block_rows), lambda i: (i, 0)),
        out_shape=jax.ShapeDtypeStruct((width // group_size, block_rows), F32),
        scratch_shapes=[
            pltpu.VMEM((blocks, groups * block_rows, seqs * LANES), BF16),
            pltpu.VMEM((blocks, 2 * block_rows, seqs * LANES), BF16),
            pltpu.VMEM((seqs, rows, LANES), BF16),
        ],
        compiler_params=params(),
        name="filter_sums",
    )(*mix_grad, product, head, front)


def input_grad_kernel(group_size, ranges, *refs):
    line_ref, back_ref, x_ref, front_ref, w_ref, filter_ref = refs[2 * ranges : 2 * ranges + 6]
    out_ref, sums_ref, band, columns, grads, inputs, edge, mix_ref, query_ref = refs[2 * ranges + 6 :]
    join(refs[:ranges], mix_ref)
    join(refs[ranges : 2 * ranges], query_ref)
    seqs, rows = mix_ref.shape[0], mix_ref.shape[1]
    block = line_ref.shape[1] // 2
    groups = LANES // group_size
    fill_band(line_ref, band, block)
    found = []
    for b in range(rows // block):
        for s in range(seqs):
            at = slice(s * LANES, (s + 1) * LANES)
            columns[b, :block, at] = mix_ref[s, b * block : (b + 1) * block]
            if (b + 1) * block < rows:
                columns[b, block:, at] = mix_ref[s, (b + 1) * block : (b + 2) * block]
            else:
                columns[b, block:, at] = back_ref[s, :block]
        stacked = jnp.dot(band[...], columns[b], preferred_element_type=F32)
        found.append(pick_groups(stacked, block, group_size))
    last = rows // block
    for s in range(seqs):
        at = slice(s * LANES, (s + 1) * LANES)
        columns[last, :HALO, at] = back_ref[s, :HALO]
        columns[last, HALO:, at] = jnp.zeros((2 * block - HALO, LANES), BF16)
    few = jnp.concatenate([band[g * block : g * block + EXTRA] for g in range(groups)], axis=0)
    stacked = jnp.dot(few, columns[last], preferred_element_type=F32)
    beyond = pick_groups(stacked, EXTRA, group_size)
    for s in range(seqs):
        at = slice(s * LANES, (s + 1) * LANES)
        after = []
        for j in (1, 2):
            own = s * 2 + j - 1
            edge[own, 0:8] = x_ref[j, s, rows - 16 :].astype(F32)[8:]
            edge[own, 8:16] = back_ref[s, HALO + EXTRA :].astype(F32)[8 * j - 8 : 8 * j]
            total = w_ref[j, 0:1] * edge[own, 8:16]
            total = total + w_ref[j, 1:2] * edge[own, 7:15]
            total = total + w_ref[j, 2:3] * edge[own, 6:14]
            after.append(total)
        streams = [
            convolve(x_ref, w_ref, inputs, j, s, front_rows(front_ref, j, s, block))
            for j in range(1, 3)
        ]
        inputs[s * 3, 0:8] = front_rows(front_ref, 0, s, block)
        inputs[s * 3, 8 : 8 + rows] = x_ref[0, s].astype(F32)
        for j in range(3):
            own = s * 3 + j
            if j == 0:
                grads[own, :rows] = query_ref[s].astype(F32)
                grads[own, rows:] = back_ref[s, HALO : HALO + EXTRA].astype(F32)[:8]
            else:
                factor = streams[2 - j]
                for b in range(rows // block):
                    part = slice(b * block, (b + 1) * block)
                    value = found[b][:, at] * factor[part]
                    grads[own, part] = value.astype(BF16).astype(F32)
                value = beyond[:8, at] * after[2 - j]
                grads[own, rows:] = value.astype(BF16).astype(F32)
            total = None
            for i in range(3):
                term = w_ref[j, i : i + 1] * grads[own, i : i + rows]
                total = term if total is None else total + term
            out_ref[j, s] = total.astype(BF16)
    for j in range(3):
        for i in range(3):
            total = None
            for s in range(seqs):
                own = s * 3 + j
                term = grads[own, :rows] * inputs[own, 8 - i : 8 - i + rows]
                term = jnp.sum(term, axis=0, keepdims=True)
                total = term if total is None else total + term
            sums_ref[0, groups + j * 3 + i : groups + j * 3 + i + 1] = total
    sums_ref[0, :groups] = filter_ref[...]
    sums_ref[0, groups + 9 :] = jnp.zeros((sums_ref.shape[1] - groups - 9, LANES), F32)


def input_grads(
    line, mix_grad, query_grad, back, x, front, short_w, filter_part, offset, group_size
):
    _, seqs, rows, _ = x.shape
    width = back.shape[2]
    block = line.shape[1] // 2
    first = offset // LANES
    groups = LANES // group_size
    local = lambda count: pl.BlockSpec((seqs, count, LANES), lambda i: (0, 0, i))
    wide3 = lambda *sizes: pl.BlockSpec(sizes + (LANES,), lambda i: (0, 0, first + i))
    wide4 = lambda *sizes: pl.BlockSpec(sizes + (LANES,), lambda i: (0, 0, 0, first + i))
    return pl.pallas_call(
        functools.partial(input_grad_kernel, group_size, len(mix_grad)),
        grid=(width // LANES,),
        in_specs=[local(part.shape[1]) for part in (*mix_grad, *query_grad)]
        + [
            pl.BlockSpec((groups, 2 * block), lambda i: (first + i, 0)),
            local(HALO + 2 * EXTRA),
            wide4(3, seqs, rows),
            wide3(seqs, front.shape[1]),
            wide3(3, 3),
            pl.BlockSpec((groups, block), lambda i: (i, 0)),
        ],
        out_specs=[
            pl.BlockSpec((3, seqs, rows, LANES), lambda i: (0, 0, 0, i)),
            pl.BlockSpec((1, groups + 16, LANES), lambda i: (i, 0, 0)),
        ],
        out_shape=[
            jax.ShapeDtypeStruct((3, seqs, rows, width), BF16),
            jax.ShapeDtypeStruct((width // LANES, groups + 16, LANES), F32),
        ],
        scratch_shapes=[
            pltpu.VMEM((groups * block, 2 * block), BF16),
            pltpu.VMEM((rows // block + 1, 2 * block, seqs * LANES), BF16),
            pltpu.VMEM((3 * seqs, rows + 8, LANES), F32),
            pltpu.VMEM((3 * seqs, rows + 8, LANES), F32),
            pltpu.VMEM((2 * seqs, 16, LANES), F32),
            pltpu.VMEM((seqs, rows, LANES), BF16),
            pltpu.VMEM((seqs, rows, LANES), BF16),
        ],
        compiler_params=params(),
        name="input_grads",
    )(*mix_grad, *query_grad, line, back, x, front, short_w, filter_part)


def total_over(block, axes):
    count = math.prod(lax.axis_size(axis) for axis in axes)
    if count & (count - 1):
        return lax.psum(block, axes)
    step = count // 2
    order = []
    while step:
        order.append(step)
        step //= 2
    for step in order:
        block = block + lax.ppermute(block, axes, [(i, i ^ step) for i in range(count)])
    return block


def shards(projected, short_w, medium_h, out_w, grad_out):
    seqs, rows, _, width = projected.shape
    taps = medium_h.shape[1]
    group_size = width // medium_h.shape[0]
    groups = LANES // group_size
    members = lax.axis_size("grp")
    cores = lax.axis_size("dp")
    length = lax.axis_size("ctx")
    partners = range(members)
    to = lambda block, k: lax.ppermute(block, "grp", [(i, i ^ k) for i in partners])
    around = lambda block: lax.ppermute(block, "ctx", [(i, (i + 1) % length) for i in range(length)])
    swap = lambda block: lax.ppermute(block, "dp", [(0, 1), (1, 0)])
    core = lax.axis_index("dp")
    pos = jnp.stack([lax.axis_index("ctx"), core, lax.axis_index("grp")]).astype(jnp.int32)

    depth = out_w.shape[0]
    ring = depth == width and cores == 2
    cut = width * FIRST // 8 if ring else depth

    def own_half(start, stop):
        half = (stop - start) // cores
        return lax.dynamic_slice_in_dim(out_w, start + core * half, half, axis=0)

    if ring:
        early, near = [around(own_half(0, cut))], [around(own_half(cut, depth))]
    else:
        whole = lax.all_gather(own_half(0, depth), ("ctx", "dp"), axis=0, tiled=True)
        weights = [Gathered(whole, members, 0)]

    x = jnp.transpose(projected, (2, 0, 1, 3))
    filters = medium_h.astype(F32)
    empty = jnp.zeros_like(filters)
    causal = jnp.concatenate([empty[:, :1], filters[:, ::-1], empty[:, 1:]], axis=1)
    anticausal = jnp.concatenate([filters, empty], axis=1)

    product, pack = products(x, short_w, taps)
    mixed_high, gated_high = mix_high(causal, product, x, short_w, taps, group_size)
    high = [gated_high] + [to(gated_high, k) for k in partners[1:]]
    if ring:
        early.append(around(after(early[-1], mixed_high)))
        near.append(around(after(near[-1], mixed_high)))
        for _ in range(length - 3):
            early.append(around(early[-1]))
            near.append(around(after(near[-1], *high[1:])))
        weights = [Passed(out_w, early, [swap(block) for block in early], 0)]

    def send_parts(piece, ranges, ready, before):
        own, parts = grad_parts(pos, after(grad_out, *ready), piece, members, ranges)
        sent = [[after(block, *before) for block in blocks] for blocks in parts]
        return own, [[to(block, k + 1) for k, block in enumerate(blocks)] for blocks in sent]

    ranges = [[(0, rows)]]
    own, got = send_parts(weights[0], ranges[0], high[1:], [])
    owns, gots = [own], [got]
    if ring:
        near[-1] = after(near[-1], *got[0][:2])
        weights.append(Passed(out_w, near, [swap(block) for block in near], cut))
        ranges.append([(0, rows)])
        own, got = send_parts(weights[1], ranges[1], [], got[0])
        owns.append(own)
        gots.append(got)

    block_out = block_output(pos, weights, high, 1, 2, None)
    front = shift(after(pack, owns[-1]), "ctx", 1)
    front = after(front, block_out)
    mixed_low, gated_low, head = mix_low(causal, front, product, x, short_w, taps, group_size)
    sent = after(gated_low, owns[-1])
    low = [gated_low] + [to(sent, k) for k in partners[1:]]

    outs, sums = [], []
    for p, piece in enumerate(weights):
        mix_grad, query_grad, back = [], [], None
        for (start, stop), terms in zip(ranges[p], gots[p]):
            held = after(owns[p], outs[-1], block_out) if p else owns[p]
            found = mix_grads(
                held,
                terms,
                start,
                stop,
                (mixed_low, mixed_high),
                x,
                front,
                short_w,
                piece.start,
            )
            mix_grad.append(found[0])
            query_grad.append(found[1])
            if start == 0:
                back = shift(found[2], "ctx", -1)
        back = after(back, *([] if p else [block_out]))
        folded = filter_sums(mix_grad, product, head, front, taps, piece.start, group_size)
        grad, part = input_grads(
            anticausal,
            mix_grad,
            query_grad,
            back,
            x,
            front,
            short_w,
            folded,
            piece.start,
            group_size,
        )
        outs.append(grad)
        sums.append(part)
    block_out = block_output(pos, weights, low, 0, 2, block_out)
    total = total_over(jnp.concatenate(sums, axis=0), ("dp", "ctx"))

    grad_projected = jnp.transpose(jnp.concatenate(outs, axis=3), (1, 2, 0, 3))
    filter_total = total[:, :groups].reshape(-1, taps)[:, ::-1]
    short_total = jnp.swapaxes(total[:, groups : groups + 9], 0, 1).reshape(3, 3, width)
    seq_total = seqs * cores
    length_total = rows * length
    filter_grad = filter_total / math.sqrt(seq_total * length_total * group_size)
    short_grad = short_total / math.sqrt(seq_total * length_total)
    return (block_out, grad_projected, filter_grad, short_grad)


def solution(mesh):
    in_specs = (
        P("dp", "ctx", None, "grp"),
        P(None, None, "grp"),
        P("grp", None),
        P("ctx", "grp"),
        P("dp", "ctx", "grp"),
    )
    out_specs = (
        P("dp", "ctx", "grp"),
        P("dp", "ctx", None, "grp"),
        P("grp", None),
        P(None, None, "grp"),
    )
    return jax.shard_map(shards, mesh=mesh, in_specs=in_specs, out_specs=out_specs, check_vma=False)
```

```python
import functools
import math

import jax
import jax.numpy as jnp
from jax import lax
from jax.experimental import pallas as pl
from jax.experimental.pallas import tpu as pltpu
from jax.sharding import PartitionSpec as P

LANES = 128
HALO = 144
FIRST = 3
EXTRA = 16
F32 = jnp.float32
BF16 = jnp.bfloat16


def params(mib=24):
    return pltpu.CompilerParams(vmem_limit_bytes=mib * 1024 * 1024)


def shift(block, axis, distance):
    devices = range(lax.axis_size(axis))
    route = [(i, i + distance) for i in devices if i + distance in devices]
    return lax.ppermute(block, axis, route)


def after(block, *others):
    return lax.optimization_barrier((block, *others))[0]


def pick_groups(stacked, rows, group_size):
    width = stacked.shape[1]
    lane = lax.broadcasted_iota(jnp.int32, (1, width), 1) % LANES
    groups = LANES // group_size
    total = stacked[:rows]
    for g in range(1, groups):
        total = jnp.where(lane >= g * group_size, stacked[g * rows : (g + 1) * rows], total)
    return total


def fill_band(line_ref, band_ref, rows):
    for g in range(line_ref.shape[0]):
        wide = jnp.broadcast_to(line_ref[g : g + 1, :], (rows, line_ref.shape[1]))
        moved = pltpu.roll(wide, 0, 1, stride=1, stride_axis=0)
        band_ref[g * rows : (g + 1) * rows, :] = moved.astype(BF16)


def convolve(x_ref, w_ref, pad, j, s, head):
    rows = x_ref.shape[2]
    own = s * 3 + j
    pad[own, 0:8] = head
    pad[own, 8 : 8 + rows] = x_ref[j, s].astype(F32)
    total = w_ref[j, 0:1] * pad[own, 8 : 8 + rows]
    total = total + w_ref[j, 1:2] * pad[own, 7 : 7 + rows]
    return total + w_ref[j, 2:3] * pad[own, 6 : 6 + rows]


def front_rows(front_ref, j, s, taps):
    return front_ref[s, taps : taps + 2 * EXTRA].astype(F32)[j * 8 : j * 8 + 8]


def product_kernel(x_ref, w_ref, product_ref, pack_ref, pad):
    seqs, rows = x_ref.shape[1], x_ref.shape[2]
    taps = pack_ref.shape[1] - 2 * EXTRA
    nothing = jnp.zeros((8, LANES), F32)
    for s in range(seqs):
        keys = convolve(x_ref, w_ref, pad, 1, s, nothing)
        values = convolve(x_ref, w_ref, pad, 2, s, nothing)
        product = (keys * values).astype(BF16)
        product_ref[s] = product
        pack_ref[s, :taps] = product[rows - taps :]
        tails = [x_ref[j, s, rows - 16 :].astype(F32)[8:] for j in range(3)]
        pack_ref[s, taps:] = jnp.concatenate(tails + [nothing], axis=0).astype(BF16)


def products(x, short_w, taps):
    _, seqs, rows, width = x.shape
    at3 = lambda i: (0, 0, i)
    return pl.pallas_call(
        product_kernel,
        grid=(width // LANES,),
        in_specs=[
            pl.BlockSpec((3, seqs, rows, LANES), lambda i: (0, 0, 0, i)),
            pl.BlockSpec((3, 3, LANES), at3),
        ],
        out_specs=[
            pl.BlockSpec((seqs, rows, LANES), at3),
            pl.BlockSpec((seqs, taps + 2 * EXTRA, LANES), at3),
        ],
        out_shape=[
            jax.ShapeDtypeStruct((seqs, rows, width), BF16),
            jax.ShapeDtypeStruct((seqs, taps + 2 * EXTRA, width), BF16),
        ],
        scratch_shapes=[pltpu.VMEM((3 * seqs, rows + 8, LANES), F32)],
        compiler_params=params(),
        name="products",
    )(x, short_w)


def mix_high_kernel(
    group_size, line_ref, low_ref, high_ref, x_ref, w_ref, mixed_ref, gated_ref, band, columns, pad
):
    seqs, rows = low_ref.shape[0], low_ref.shape[1]
    fill_band(line_ref, band, rows)
    for s in range(seqs):
        at = slice(s * LANES, (s + 1) * LANES)
        columns[:rows, at] = low_ref[s]
        columns[rows:, at] = high_ref[s]
    stacked = jnp.dot(band[...], columns[...], preferred_element_type=F32)
    mixed = pick_groups(stacked, rows, group_size)
    nothing = jnp.zeros((8, LANES), F32)
    for s in range(seqs):
        part = mixed[:, s * LANES : (s + 1) * LANES]
        mixed_ref[s] = part
        query = convolve(x_ref, w_ref, pad, 0, s, nothing)[rows:]
        gated_ref[s] = (query * part).astype(BF16)


def mix_high(line, product, x, short_w, rows, group_size):
    _, seqs, length, width = x.shape
    groups = LANES // group_size
    part = lambda at: pl.BlockSpec((seqs, rows, LANES), lambda i: (0, at, i))
    shape = (seqs, rows, width)
    return pl.pallas_call(
        functools.partial(mix_high_kernel, group_size),
        grid=(width // LANES,),
        in_specs=[
            pl.BlockSpec((groups, 2 * rows), lambda i: (i, 0)),
            part(0),
            part(1),
            pl.BlockSpec((1, seqs, length, LANES), lambda i: (0, 0, 0, i)),
            pl.BlockSpec((3, 3, LANES), lambda i: (0, 0, i)),
        ],
        out_specs=[part(0), part(0)],
        out_shape=[jax.ShapeDtypeStruct(shape, F32), jax.ShapeDtypeStruct(shape, BF16)],
        scratch_shapes=[
            pltpu.VMEM((groups * rows, 2 * rows), BF16),
            pltpu.VMEM((2 * rows, seqs * LANES), BF16),
            pltpu.VMEM((3 * seqs, length + 8, LANES), F32),
        ],
        compiler_params=params(),
        name="mix_high",
    )(line, product, product, x, short_w)


def mix_low_kernel(
    group_size,
    line_ref,
    front_ref,
    product_ref,
    x_ref,
    w_ref,
    mixed_ref,
    gated_ref,
    head_ref,
    band,
    columns,
    pad,
):
    seqs, rows = product_ref.shape[0], product_ref.shape[1]
    fill_band(line_ref, band, rows)
    queries = []
    for s in range(seqs):
        at = slice(s * LANES, (s + 1) * LANES)
        found = [
            convolve(x_ref, w_ref, pad, j, s, front_rows(front_ref, j, s, rows)) for j in range(3)
        ]
        queries.append(found[0])
        head = (found[1][:EXTRA] * found[2][:EXTRA]).astype(BF16)
        head_ref[s] = head
        columns[:rows, at] = front_ref[s, :rows]
        columns[rows : rows + EXTRA, at] = head
        columns[rows + EXTRA :, at] = product_ref[s, EXTRA:]
    stacked = jnp.dot(band[...], columns[...], preferred_element_type=F32)
    mixed = pick_groups(stacked, rows, group_size)
    for s in range(seqs):
        part = mixed[:, s * LANES : (s + 1) * LANES]
        mixed_ref[s] = part
        gated_ref[s] = (queries[s] * part).astype(BF16)


def mix_low(line, front, product, x, short_w, rows, group_size):
    _, seqs, _, width = x.shape
    groups = LANES // group_size
    part = lambda count: pl.BlockSpec((seqs, count, LANES), lambda i: (0, 0, i))
    shape = (seqs, rows, width)
    return pl.pallas_call(
        functools.partial(mix_low_kernel, group_size),
        grid=(width // LANES,),
        in_specs=[
            pl.BlockSpec((groups, 2 * rows), lambda i: (i, 0)),
            part(front.shape[1]),
            part(rows),
            pl.BlockSpec((3, seqs, rows, LANES), lambda i: (0, 0, 0, i)),
            pl.BlockSpec((3, 3, LANES), lambda i: (0, 0, i)),
        ],
        out_specs=[part(rows), part(rows), part(EXTRA)],
        out_shape=[
            jax.ShapeDtypeStruct(shape, F32),
            jax.ShapeDtypeStruct(shape, BF16),
            jax.ShapeDtypeStruct((seqs, EXTRA, width), BF16),
        ],
        scratch_shapes=[
            pltpu.VMEM((groups * rows, 2 * rows), BF16),
            pltpu.VMEM((2 * rows, seqs * LANES), BF16),
            pltpu.VMEM((3 * seqs, rows + 8, LANES), F32),
        ],
        compiler_params=params(),
        name="mix_low",
    )(line, front, product, x, short_w)


class Gathered:
    def __init__(self, w, steps, start):
        self.arrays, self.start, self.span = [w], start, w.shape[0] // steps

    def fetch(self, pos_ref, refs, buffer, base, sems, partner):
        owner = lax.bitwise_xor(pos_ref[2], partner)
        rows = pl.ds(pl.multiple_of(owner * self.span, self.span), self.span)
        place = buffer.at[partner, pl.ds(base, self.span)]
        copy = pltpu.make_async_copy(refs[0].at[rows], place, sems.at[partner, 0])
        copy.start()
        return [copy]


class Passed:
    def __init__(self, own, near, far, start):
        self.arrays, self.start, self.span = [own, *near, *far], start, 2 * near[0].shape[0]

    def fetch(self, pos_ref, refs, buffer, base, sems, partner):
        steps, half = (len(refs) + 1) // 2, self.span // 2
        owner = lax.bitwise_xor(pos_ref[2], partner)
        step = lax.rem(pos_ref[0] - owner + steps, steps)
        mine = pl.multiple_of(pos_ref[1] * half, half)
        other = pl.multiple_of((1 - pos_ref[1]) * half, half)

        def copies(first, second):
            return [
                pltpu.make_async_copy(
                    source, buffer.at[partner, pl.ds(base + place, half)], sems.at[partner, which]
                )
                for which, (source, place) in enumerate(((first, mine), (second, other)))
            ]

        for distance in range(steps):

            @pl.when(step == distance)
            def _(distance=distance):
                if distance == 0:
                    pair = [refs[0].at[pl.ds(self.start + at, half)] for at in (mine, other)]
                else:
                    pair = [refs[distance], refs[steps - 1 + distance]]
                for copy in copies(*pair):
                    copy.start()

        return copies(refs[1], refs[steps])


def grad_kernel(weights, steps, ranges, pos_ref, cot_ref, *refs):
    held = len(weights.arrays)
    outs, (buffer, sems) = refs[held:-2], refs[-2:]
    order = list(range(1, steps)) + [0]
    copies = {
        partner: weights.fetch(pos_ref, refs[:held], buffer, 0, sems, partner)
        for partner in order
    }
    for partner in order:
        for copy in copies[partner]:
            copy.wait()
        part = lax.dot_general(
            cot_ref[...],
            buffer[partner],
            (((1,), (1,)), ((), ())),
            preferred_element_type=F32,
        )
        if partner == 0:
            outs[0][...] = part.reshape(outs[0].shape)
            continue
        for r, (start, stop) in enumerate(ranges):
            out_ref = outs[1 + r * (steps - 1) + partner - 1]
            rows = outs[0].shape[1]
            for s in range(out_ref.shape[0]):
                out_ref[s] = part[s * rows + start : s * rows + stop].astype(BF16)


def grad_parts(pos, cotangent, weights, steps, ranges):
    seqs, rows, width = cotangent.shape
    span = weights.span
    inside = pl.BlockSpec(memory_space=pltpu.VMEM)
    shapes = [jax.ShapeDtypeStruct((seqs, rows, span), F32)]
    for start, stop in ranges:
        shapes += [jax.ShapeDtypeStruct((seqs, stop - start, span), BF16)] * (steps - 1)
    found = pl.pallas_call(
        functools.partial(grad_kernel, weights, steps, ranges),
        in_specs=[pl.BlockSpec(memory_space=pltpu.SMEM), inside]
        + [pl.BlockSpec(memory_space=pltpu.HBM)] * len(weights.arrays),
        out_specs=[inside] * len(shapes),
        out_shape=shapes,
        scratch_shapes=[
            pltpu.VMEM((steps, span, width), BF16),
            pltpu.SemaphoreType.DMA((steps, 2)),
        ],
        compiler_params=params(24),
        name="grad_parts",
    )(pos, cotangent.reshape(seqs * rows, width), *weights.arrays)
    return found[0], [
        found[1 + r * (steps - 1) : 1 + (r + 1) * (steps - 1)] for r in range(len(ranges))
    ]


def out_kernel(weights, steps, pos_ref, *refs):
    out_ref, buffer, *sems = refs[-2 - len(weights) :]
    copies = {partner: [] for partner in range(steps)}
    for piece, piece_sems in zip(weights, sems):
        held, refs = refs[: len(piece.arrays)], refs[len(piece.arrays) :]
        for partner in range(steps):
            copies[partner] += piece.fetch(
                pos_ref, held, buffer, piece.start, piece_sems, partner
            )
    total = None
    for partner in range(steps):
        for copy in copies[partner]:
            copy.wait()
        left = refs[partner][...].reshape(-1, buffer.shape[1])
        term = jnp.dot(left, buffer[partner], preferred_element_type=F32)
        total = term if total is None else total + term
    out_ref[...] = total.astype(BF16).reshape(out_ref.shape)


def block_output(pos, weights, gated, at, blocks, before):
    steps = len(gated)
    seqs, rows, depth = gated[0].shape
    width = weights[0].arrays[0].shape[1]
    inside = pl.BlockSpec(memory_space=pltpu.VMEM)
    anywhere = pl.BlockSpec(memory_space=pltpu.HBM)
    arrays = [array for piece in weights for array in piece.arrays]
    before = [] if before is None else [before]
    return pl.pallas_call(
        functools.partial(out_kernel, weights, steps),
        grid=(1,),
        in_specs=[pl.BlockSpec(memory_space=pltpu.SMEM)]
        + [anywhere] * len(arrays)
        + [inside] * steps
        + [anywhere] * len(before),
        out_specs=pl.BlockSpec((seqs, rows, width), lambda i: (0, at, 0)),
        out_shape=jax.ShapeDtypeStruct((seqs, blocks * rows, width), BF16),
        scratch_shapes=[pltpu.VMEM((steps, depth, width), BF16)]
        + [pltpu.SemaphoreType.DMA((steps, 2))] * len(weights),
        input_output_aliases={1 + len(arrays) + steps: 0} if before else {},
        compiler_params=params(24),
        name="block_output",
    )(pos, *arrays, *gated, *before)


def mix_grad_kernel(count, start, stop, *refs):
    terms = refs[:count]
    low_ref, high_ref, x_ref, front_ref, w_ref, mix_ref, query_ref = refs[count : count + 7]
    pad = refs[-1]
    seqs, half = x_ref.shape[1], low_ref.shape[1]
    for s in range(seqs):
        query = convolve(x_ref, w_ref, pad, 0, s, front_rows(front_ref, 0, s, half))
        for first, mixed_ref in ((0, low_ref), (half, high_ref)):
            begin, end = max(first, start), min(first + half, stop)
            if begin >= end:
                continue
            at = slice(begin - start, end - start)
            total = terms[0][s, begin:end]
            for term in terms[1:]:
                total = total + term[s, at].astype(F32)
            gated_grad = total.astype(BF16).astype(F32)
            mixed = mixed_ref[s, begin - first : end - first]
            mix_ref[s, at] = (gated_grad * query[begin:end]).astype(BF16)
            query_ref[s, at] = (gated_grad * mixed).astype(BF16)
        if start == 0:
            pack_ref = refs[count + 7]
            pack_ref[s, :HALO] = mix_ref[s, :HALO]
            pack_ref[s, HALO : HALO + EXTRA] = query_ref[s, :EXTRA]
            heads = [x_ref[j, s, :EXTRA].astype(F32)[:8] for j in (1, 2)]
            pack_ref[s, HALO + EXTRA :] = jnp.concatenate(heads, axis=0).astype(BF16)


def mix_grads(own, terms, start, stop, mixed, x, front, short_w, offset):
    seqs, rows, width = own.shape
    half = rows // 2
    first = offset // LANES
    local = lambda count: pl.BlockSpec((seqs, count, LANES), lambda i: (0, 0, i))
    wide = lambda count: pl.BlockSpec((seqs, count, LANES), lambda i: (0, 0, first + i))
    counts = [stop - start] * 2 + [HALO + 2 * EXTRA] * (start == 0)
    return pl.pallas_call(
        functools.partial(mix_grad_kernel, 1 + len(terms), start, stop),
        grid=(width // LANES,),
        in_specs=[local(rows)]
        + [local(stop - start)] * len(terms)
        + [wide(half), wide(half)]
        + [
            pl.BlockSpec((3, seqs, rows, LANES), lambda i: (0, 0, 0, first + i)),
            wide(front.shape[1]),
            pl.BlockSpec((3, 3, LANES), lambda i: (0, 0, first + i)),
        ],
        out_specs=[local(count) for count in counts],
        out_shape=[jax.ShapeDtypeStruct((seqs, count, width), BF16) for count in counts],
        scratch_shapes=[pltpu.VMEM((3 * seqs, rows + 8, LANES), F32)],
        compiler_params=params(),
        name="mix_grads",
    )(own, *terms, *mixed, x, front, short_w)


def join(parts, whole_ref):
    at = 0
    for part_ref in parts:
        whole_ref[:, at : at + part_ref.shape[1]] = part_ref[...]
        at += part_ref.shape[1]


def filter_kernel(group_size, ranges, *refs):
    product_ref, head_ref, front_ref, out_ref, left, columns, mix_ref = refs[ranges:]
    join(refs[:ranges], mix_ref)
    seqs = mix_ref.shape[0]
    rows = out_ref.shape[1]
    groups = LANES // group_size
    lane = lax.broadcasted_iota(jnp.int32, (1, LANES), 1) // group_size
    total = None
    for b in range(mix_ref.shape[1] // rows):
        for s in range(seqs):
            at = slice(s * LANES, (s + 1) * LANES)
            block = mix_ref[s, b * rows : (b + 1) * rows]
            for g in range(groups):
                keep = (lane == g).astype(F32).astype(BF16)
                left[b, g * rows : (g + 1) * rows, at] = block * keep
            if b == 0:
                columns[b, :rows, at] = front_ref[s, :rows]
            else:
                columns[b, :rows, at] = product_ref[s, (b - 1) * rows : b * rows]
            columns[b, rows:, at] = product_ref[s, b * rows : (b + 1) * rows]
            if b < 2:
                start = (1 - b) * rows
                columns[b, start : start + EXTRA, at] = head_ref[s]
        term = lax.dot_general(
            left[b], columns[b], (((1,), (1,)), ((), ())), preferred_element_type=F32
        )
        total = term if total is None else total + term
    span = 2 * rows
    folded = []
    for g in range(groups):
        sum_g = None
        for a in range(rows // 8):
            tile = total[g * rows + a * 8 : g * rows + a * 8 + 8]
            tile = pltpu.roll(tile, (span - a * 8) % span, 1)
            sum_g = tile if sum_g is None else sum_g + tile
        folded.append(sum_g)
    stacked = jnp.stack(folded, axis=0)
    result = None
    for r in range(8):
        row = pltpu.roll(stacked[:, r, :], span - r - 1, 1)
        result = row if result is None else result + row
    out_ref[...] = result[:, :rows]


def filter_sums(mix_grad, product, head, front, block_rows, offset, group_size):
    seqs, rows, _ = product.shape
    width = mix_grad[0].shape[2]
    first = offset // LANES
    groups = LANES // group_size
    blocks = rows // block_rows
    return pl.pallas_call(
        functools.partial(filter_kernel, group_size, len(mix_grad)),
        grid=(width // LANES,),
        in_specs=[
            pl.BlockSpec((seqs, part.shape[1], LANES), lambda i: (0, 0, i)) for part in mix_grad
        ]
        + [
            pl.BlockSpec((seqs, rows, LANES), lambda i: (0, 0, first + i)),
            pl.BlockSpec((seqs, EXTRA, LANES), lambda i: (0, 0, first + i)),
            pl.BlockSpec((seqs, front.shape[1], LANES), lambda i: (0, 0, first + i)),
        ],
        out_specs=pl.BlockSpec((groups, block_rows), lambda i: (i, 0)),
        out_shape=jax.ShapeDtypeStruct((width // group_size, block_rows), F32),
        scratch_shapes=[
            pltpu.VMEM((blocks, groups * block_rows, seqs * LANES), BF16),
            pltpu.VMEM((blocks, 2 * block_rows, seqs * LANES), BF16),
            pltpu.VMEM((seqs, rows, LANES), BF16),
        ],
        compiler_params=params(),
        name="filter_sums",
    )(*mix_grad, product, head, front)


def input_grad_kernel(group_size, ranges, *refs):
    line_ref, back_ref, x_ref, front_ref, w_ref, filter_ref = refs[2 * ranges : 2 * ranges + 6]
    out_ref, sums_ref, band, columns, grads, inputs, edge, mix_ref, query_ref = refs[2 * ranges + 6 :]
    join(refs[:ranges], mix_ref)
    join(refs[ranges : 2 * ranges], query_ref)
    seqs, rows = mix_ref.shape[0], mix_ref.shape[1]
    block = line_ref.shape[1] // 2
    groups = LANES // group_size
    fill_band(line_ref, band, block)
    found = []
    for b in range(rows // block):
        for s in range(seqs):
            at = slice(s * LANES, (s + 1) * LANES)
            columns[b, :block, at] = mix_ref[s, b * block : (b + 1) * block]
            if (b + 1) * block < rows:
                columns[b, block:, at] = mix_ref[s, (b + 1) * block : (b + 2) * block]
            else:
                columns[b, block:, at] = back_ref[s, :block]
        stacked = jnp.dot(band[...], columns[b], preferred_element_type=F32)
        found.append(pick_groups(stacked, block, group_size))
    last = rows // block
    for s in range(seqs):
        at = slice(s * LANES, (s + 1) * LANES)
        columns[last, :HALO, at] = back_ref[s, :HALO]
        columns[last, HALO:, at] = jnp.zeros((2 * block - HALO, LANES), BF16)
    few = jnp.concatenate([band[g * block : g * block + EXTRA] for g in range(groups)], axis=0)
    stacked = jnp.dot(few, columns[last], preferred_element_type=F32)
    beyond = pick_groups(stacked, EXTRA, group_size)
    for s in range(seqs):
        at = slice(s * LANES, (s + 1) * LANES)
        after = []
        for j in (1, 2):
            own = s * 2 + j - 1
            edge[own, 0:8] = x_ref[j, s, rows - 16 :].astype(F32)[8:]
            edge[own, 8:16] = back_ref[s, HALO + EXTRA :].astype(F32)[8 * j - 8 : 8 * j]
            total = w_ref[j, 0:1] * edge[own, 8:16]
            total = total + w_ref[j, 1:2] * edge[own, 7:15]
            total = total + w_ref[j, 2:3] * edge[own, 6:14]
            after.append(total)
        streams = [
            convolve(x_ref, w_ref, inputs, j, s, front_rows(front_ref, j, s, block))
            for j in range(1, 3)
        ]
        inputs[s * 3, 0:8] = front_rows(front_ref, 0, s, block)
        inputs[s * 3, 8 : 8 + rows] = x_ref[0, s].astype(F32)
        for j in range(3):
            own = s * 3 + j
            if j == 0:
                grads[own, :rows] = query_ref[s].astype(F32)
                grads[own, rows:] = back_ref[s, HALO : HALO + EXTRA].astype(F32)[:8]
            else:
                factor = streams[2 - j]
                for b in range(rows // block):
                    part = slice(b * block, (b + 1) * block)
                    value = found[b][:, at] * factor[part]
                    grads[own, part] = value.astype(BF16).astype(F32)
                value = beyond[:8, at] * after[2 - j]
                grads[own, rows:] = value.astype(BF16).astype(F32)
            total = None
            for i in range(3):
                term = w_ref[j, i : i + 1] * grads[own, i : i + rows]
                total = term if total is None else total + term
            out_ref[j, s] = total.astype(BF16)
    for j in range(3):
        for i in range(3):
            total = None
            for s in range(seqs):
                own = s * 3 + j
                term = grads[own, :rows] * inputs[own, 8 - i : 8 - i + rows]
                term = jnp.sum(term, axis=0, keepdims=True)
                total = term if total is None else total + term
            sums_ref[0, groups + j * 3 + i : groups + j * 3 + i + 1] = total
    sums_ref[0, :groups] = filter_ref[...]
    sums_ref[0, groups + 9 :] = jnp.zeros((sums_ref.shape[1] - groups - 9, LANES), F32)


def input_grads(
    line, mix_grad, query_grad, back, x, front, short_w, filter_part, offset, group_size
):
    _, seqs, rows, _ = x.shape
    width = back.shape[2]
    block = line.shape[1] // 2
    first = offset // LANES
    groups = LANES // group_size
    local = lambda count: pl.BlockSpec((seqs, count, LANES), lambda i: (0, 0, i))
    wide3 = lambda *sizes: pl.BlockSpec(sizes + (LANES,), lambda i: (0, 0, first + i))
    wide4 = lambda *sizes: pl.BlockSpec(sizes + (LANES,), lambda i: (0, 0, 0, first + i))
    return pl.pallas_call(
        functools.partial(input_grad_kernel, group_size, len(mix_grad)),
        grid=(width // LANES,),
        in_specs=[local(part.shape[1]) for part in (*mix_grad, *query_grad)]
        + [
            pl.BlockSpec((groups, 2 * block), lambda i: (first + i, 0)),
            local(HALO + 2 * EXTRA),
            wide4(3, seqs, rows),
            wide3(seqs, front.shape[1]),
            wide3(3, 3),
            pl.BlockSpec((groups, block), lambda i: (i, 0)),
        ],
        out_specs=[
            pl.BlockSpec((3, seqs, rows, LANES), lambda i: (0, 0, 0, i)),
            pl.BlockSpec((1, groups + 16, LANES), lambda i: (i, 0, 0)),
        ],
        out_shape=[
            jax.ShapeDtypeStruct((3, seqs, rows, width), BF16),
            jax.ShapeDtypeStruct((width // LANES, groups + 16, LANES), F32),
        ],
        scratch_shapes=[
            pltpu.VMEM((groups * block, 2 * block), BF16),
            pltpu.VMEM((rows // block + 1, 2 * block, seqs * LANES), BF16),
            pltpu.VMEM((3 * seqs, rows + 8, LANES), F32),
            pltpu.VMEM((3 * seqs, rows + 8, LANES), F32),
            pltpu.VMEM((2 * seqs, 16, LANES), F32),
            pltpu.VMEM((seqs, rows, LANES), BF16),
            pltpu.VMEM((seqs, rows, LANES), BF16),
        ],
        compiler_params=params(),
        name="input_grads",
    )(*mix_grad, *query_grad, line, back, x, front, short_w, filter_part)


def total_over(block, axes):
    count = math.prod(lax.axis_size(axis) for axis in axes)
    if count & (count - 1):
        return lax.psum(block, axes)
    step = count // 2
    order = []
    while step:
        order.append(step)
        step //= 2
    for step in order:
        block = block + lax.ppermute(block, axes, [(i, i ^ step) for i in range(count)])
    return block


def shards(projected, short_w, medium_h, out_w, grad_out):
    seqs, rows, _, width = projected.shape
    taps = medium_h.shape[1]
    group_size = width // medium_h.shape[0]
    groups = LANES // group_size
    members = lax.axis_size("grp")
    cores = lax.axis_size("dp")
    length = lax.axis_size("ctx")
    partners = range(members)
    to = lambda block, k: lax.ppermute(block, "grp", [(i, i ^ k) for i in partners])
    around = lambda block: lax.ppermute(block, "ctx", [(i, (i + 1) % length) for i in range(length)])
    swap = lambda block: lax.ppermute(block, "dp", [(0, 1), (1, 0)])
    core = lax.axis_index("dp")
    pos = jnp.stack([lax.axis_index("ctx"), core, lax.axis_index("grp")]).astype(jnp.int32)

    depth = out_w.shape[0]
    ring = depth == width and cores == 2
    cut = width * FIRST // 8 if ring else depth

    def own_half(start, stop):
        half = (stop - start) // cores
        return lax.dynamic_slice_in_dim(out_w, start + core * half, half, axis=0)

    if ring:
        early, near = [around(own_half(0, cut))], [around(own_half(cut, depth))]
    else:
        whole = lax.all_gather(own_half(0, depth), ("ctx", "dp"), axis=0, tiled=True)
        weights = [Gathered(whole, members, 0)]

    x = jnp.transpose(projected, (2, 0, 1, 3))
    filters = medium_h.astype(F32)
    empty = jnp.zeros_like(filters)
    causal = jnp.concatenate([empty[:, :1], filters[:, ::-1], empty[:, 1:]], axis=1)
    anticausal = jnp.concatenate([filters, empty], axis=1)

    product, pack = products(x, short_w, taps)
    mixed_high, gated_high = mix_high(causal, product, x, short_w, taps, group_size)
    high = [gated_high] + [to(gated_high, k) for k in partners[1:]]
    if ring:
        early.append(around(after(early[-1], mixed_high)))
        near.append(around(after(near[-1], mixed_high)))
        for _ in range(length - 3):
            early.append(around(early[-1]))
            near.append(around(after(near[-1], *high[1:])))
        weights = [Passed(out_w, early, [swap(block) for block in early], 0)]

    def send_parts(piece, ranges, ready, before):
        own, parts = grad_parts(pos, after(grad_out, *ready), piece, members, ranges)
        sent = [[after(block, *before) for block in blocks] for blocks in parts]
        return own, [[to(block, k + 1) for k, block in enumerate(blocks)] for blocks in sent]

    ranges = [[(0, rows)]]
    own, got = send_parts(weights[0], ranges[0], high[1:], [])
    owns, gots = [own], [got]
    if ring:
        near[-1] = after(near[-1], *got[0][:2])
        weights.append(Passed(out_w, near, [swap(block) for block in near], cut))
        ranges.append([(0, rows)])
        own, got = send_parts(weights[1], ranges[1], [], got[0])
        owns.append(own)
        gots.append(got)

    block_out = block_output(pos, weights, high, 1, 2, None)
    front = shift(after(pack, owns[0]), "ctx", 1)
    front = after(front, block_out)
    mixed_low, gated_low, head = mix_low(causal, front, product, x, short_w, taps, group_size)
    sent = after(gated_low, owns[-1])
    low = [gated_low] + [to(sent, k) for k in partners[1:]]

    outs, sums = [], []
    for p, piece in enumerate(weights):
        mix_grad, query_grad, back = [], [], None
        for (start, stop), terms in zip(ranges[p], gots[p]):
            held = after(owns[p], outs[-1], block_out) if p else owns[p]
            found = mix_grads(
                held,
                terms,
                start,
                stop,
                (mixed_low, mixed_high),
                x,
                front,
                short_w,
                piece.start,
            )
            mix_grad.append(found[0])
            query_grad.append(found[1])
            if start == 0:
                back = shift(found[2], "ctx", -1)
        back = after(back, *([] if p else [block_out]))
        folded = filter_sums(mix_grad, product, head, front, taps, piece.start, group_size)
        grad, part = input_grads(
            anticausal,
            mix_grad,
            query_grad,
            back,
            x,
            front,
            short_w,
            folded,
            piece.start,
            group_size,
        )
        outs.append(grad)
        sums.append(part)
    block_out = block_output(pos, weights, low, 0, 2, block_out)
    total = total_over(jnp.concatenate(sums, axis=0), ("dp", "ctx"))

    grad_projected = jnp.transpose(jnp.concatenate(outs, axis=3), (1, 2, 0, 3))
    filter_total = total[:, :groups].reshape(-1, taps)[:, ::-1]
    short_total = jnp.swapaxes(total[:, groups : groups + 9], 0, 1).reshape(3, 3, width)
    seq_total = seqs * cores
    length_total = rows * length
    filter_grad = filter_total / math.sqrt(seq_total * length_total * group_size)
    short_grad = short_total / math.sqrt(seq_total * length_total)
    return (block_out, grad_projected, filter_grad, short_grad)


def solution(mesh):
    in_specs = (
        P("dp", "ctx", None, "grp"),
        P(None, None, "grp"),
        P("grp", None),
        P("ctx", "grp"),
        P("dp", "ctx", "grp"),
    )
    out_specs = (
        P("dp", "ctx", "grp"),
        P("dp", "ctx", None, "grp"),
        P("grp", None),
        P(None, None, "grp"),
    )
    return jax.shard_map(shards, mesh=mesh, in_specs=in_specs, out_specs=out_specs, check_vma=False)
```

```python
import functools
import math

import jax
import jax.numpy as jnp
from jax import lax
from jax.experimental import pallas as pl
from jax.experimental.pallas import tpu as pltpu
from jax.sharding import PartitionSpec as P

LANES = 128
HALO = 144
FIRST = 3
EXTRA = 16
F32 = jnp.float32
BF16 = jnp.bfloat16


def params(mib=24):
    return pltpu.CompilerParams(vmem_limit_bytes=mib * 1024 * 1024)


def shift(block, axis, distance):
    devices = range(lax.axis_size(axis))
    route = [(i, i + distance) for i in devices if i + distance in devices]
    return lax.ppermute(block, axis, route)


def after(block, *others):
    return lax.optimization_barrier((block, *others))[0]


def pick_groups(stacked, rows, group_size):
    width = stacked.shape[1]
    lane = lax.broadcasted_iota(jnp.int32, (1, width), 1) % LANES
    groups = LANES // group_size
    total = stacked[:rows]
    for g in range(1, groups):
        total = jnp.where(lane >= g * group_size, stacked[g * rows : (g + 1) * rows], total)
    return total


def fill_band(line_ref, band_ref, rows):
    for g in range(line_ref.shape[0]):
        wide = jnp.broadcast_to(line_ref[g : g + 1, :], (rows, line_ref.shape[1]))
        moved = pltpu.roll(wide, 0, 1, stride=1, stride_axis=0)
        band_ref[g * rows : (g + 1) * rows, :] = moved.astype(BF16)


def convolve(x_ref, w_ref, pad, j, s, head):
    rows = x_ref.shape[2]
    own = s * 3 + j
    pad[own, 0:8] = head
    pad[own, 8 : 8 + rows] = x_ref[j, s].astype(F32)
    total = w_ref[j, 0:1] * pad[own, 8 : 8 + rows]
    total = total + w_ref[j, 1:2] * pad[own, 7 : 7 + rows]
    return total + w_ref[j, 2:3] * pad[own, 6 : 6 + rows]


def front_rows(front_ref, j, s, taps):
    return front_ref[s, taps : taps + 2 * EXTRA].astype(F32)[j * 8 : j * 8 + 8]


def product_kernel(x_ref, w_ref, product_ref, pack_ref, pad):
    seqs, rows = x_ref.shape[1], x_ref.shape[2]
    taps = pack_ref.shape[1] - 2 * EXTRA
    nothing = jnp.zeros((8, LANES), F32)
    for s in range(seqs):
        keys = convolve(x_ref, w_ref, pad, 1, s, nothing)
        values = convolve(x_ref, w_ref, pad, 2, s, nothing)
        product = (keys * values).astype(BF16)
        product_ref[s] = product
        pack_ref[s, :taps] = product[rows - taps :]
        tails = [x_ref[j, s, rows - 16 :].astype(F32)[8:] for j in range(3)]
        pack_ref[s, taps:] = jnp.concatenate(tails + [nothing], axis=0).astype(BF16)


def products(x, short_w, taps):
    _, seqs, rows, width = x.shape
    at3 = lambda i: (0, 0, i)
    return pl.pallas_call(
        product_kernel,
        grid=(width // LANES,),
        in_specs=[
            pl.BlockSpec((3, seqs, rows, LANES), lambda i: (0, 0, 0, i)),
            pl.BlockSpec((3, 3, LANES), at3),
        ],
        out_specs=[
            pl.BlockSpec((seqs, rows, LANES), at3),
            pl.BlockSpec((seqs, taps + 2 * EXTRA, LANES), at3),
        ],
        out_shape=[
            jax.ShapeDtypeStruct((seqs, rows, width), BF16),
            jax.ShapeDtypeStruct((seqs, taps + 2 * EXTRA, width), BF16),
        ],
        scratch_shapes=[pltpu.VMEM((3 * seqs, rows + 8, LANES), F32)],
        compiler_params=params(),
        name="products",
    )(x, short_w)


def mix_high_kernel(
    group_size, line_ref, low_ref, high_ref, x_ref, w_ref, mixed_ref, gated_ref, band, columns, pad
):
    seqs, rows = low_ref.shape[0], low_ref.shape[1]
    fill_band(line_ref, band, rows)
    for s in range(seqs):
        at = slice(s * LANES, (s + 1) * LANES)
        columns[:rows, at] = low_ref[s]
        columns[rows:, at] = high_ref[s]
    stacked = jnp.dot(band[...], columns[...], preferred_element_type=F32)
    mixed = pick_groups(stacked, rows, group_size)
    nothing = jnp.zeros((8, LANES), F32)
    for s in range(seqs):
        part = mixed[:, s * LANES : (s + 1) * LANES]
        mixed_ref[s] = part
        query = convolve(x_ref, w_ref, pad, 0, s, nothing)[rows:]
        gated_ref[s] = (query * part).astype(BF16)


def mix_high(line, product, x, short_w, rows, group_size):
    _, seqs, length, width = x.shape
    groups = LANES // group_size
    part = lambda at: pl.BlockSpec((seqs, rows, LANES), lambda i: (0, at, i))
    shape = (seqs, rows, width)
    return pl.pallas_call(
        functools.partial(mix_high_kernel, group_size),
        grid=(width // LANES,),
        in_specs=[
            pl.BlockSpec((groups, 2 * rows), lambda i: (i, 0)),
            part(0),
            part(1),
            pl.BlockSpec((1, seqs, length, LANES), lambda i: (0, 0, 0, i)),
            pl.BlockSpec((3, 3, LANES), lambda i: (0, 0, i)),
        ],
        out_specs=[part(0), part(0)],
        out_shape=[jax.ShapeDtypeStruct(shape, F32), jax.ShapeDtypeStruct(shape, BF16)],
        scratch_shapes=[
            pltpu.VMEM((groups * rows, 2 * rows), BF16),
            pltpu.VMEM((2 * rows, seqs * LANES), BF16),
            pltpu.VMEM((3 * seqs, length + 8, LANES), F32),
        ],
        compiler_params=params(),
        name="mix_high",
    )(line, product, product, x, short_w)


def mix_low_kernel(
    group_size,
    line_ref,
    front_ref,
    product_ref,
    x_ref,
    w_ref,
    mixed_ref,
    gated_ref,
    head_ref,
    band,
    columns,
    pad,
):
    seqs, rows = product_ref.shape[0], product_ref.shape[1]
    fill_band(line_ref, band, rows)
    queries = []
    for s in range(seqs):
        at = slice(s * LANES, (s + 1) * LANES)
        found = [
            convolve(x_ref, w_ref, pad, j, s, front_rows(front_ref, j, s, rows)) for j in range(3)
        ]
        queries.append(found[0])
        head = (found[1][:EXTRA] * found[2][:EXTRA]).astype(BF16)
        head_ref[s] = head
        columns[:rows, at] = front_ref[s, :rows]
        columns[rows : rows + EXTRA, at] = head
        columns[rows + EXTRA :, at] = product_ref[s, EXTRA:]
    stacked = jnp.dot(band[...], columns[...], preferred_element_type=F32)
    mixed = pick_groups(stacked, rows, group_size)
    for s in range(seqs):
        part = mixed[:, s * LANES : (s + 1) * LANES]
        mixed_ref[s] = part
        gated_ref[s] = (queries[s] * part).astype(BF16)


def mix_low(line, front, product, x, short_w, rows, group_size):
    _, seqs, _, width = x.shape
    groups = LANES // group_size
    part = lambda count: pl.BlockSpec((seqs, count, LANES), lambda i: (0, 0, i))
    shape = (seqs, rows, width)
    return pl.pallas_call(
        functools.partial(mix_low_kernel, group_size),
        grid=(width // LANES,),
        in_specs=[
            pl.BlockSpec((groups, 2 * rows), lambda i: (i, 0)),
            part(front.shape[1]),
            part(rows),
            pl.BlockSpec((3, seqs, rows, LANES), lambda i: (0, 0, 0, i)),
            pl.BlockSpec((3, 3, LANES), lambda i: (0, 0, i)),
        ],
        out_specs=[part(rows), part(rows), part(EXTRA)],
        out_shape=[
            jax.ShapeDtypeStruct(shape, F32),
            jax.ShapeDtypeStruct(shape, BF16),
            jax.ShapeDtypeStruct((seqs, EXTRA, width), BF16),
        ],
        scratch_shapes=[
            pltpu.VMEM((groups * rows, 2 * rows), BF16),
            pltpu.VMEM((2 * rows, seqs * LANES), BF16),
            pltpu.VMEM((3 * seqs, rows + 8, LANES), F32),
        ],
        compiler_params=params(),
        name="mix_low",
    )(line, front, product, x, short_w)


class Gathered:
    def __init__(self, w, steps, start):
        self.arrays, self.start, self.span = [w], start, w.shape[0] // steps

    def fetch(self, pos_ref, refs, buffer, base, sems, partner):
        owner = lax.bitwise_xor(pos_ref[2], partner)
        rows = pl.ds(pl.multiple_of(owner * self.span, self.span), self.span)
        place = buffer.at[partner, pl.ds(base, self.span)]
        copy = pltpu.make_async_copy(refs[0].at[rows], place, sems.at[partner, 0])
        copy.start()
        return [copy]


class Passed:
    def __init__(self, own, near, far, start):
        self.arrays, self.start, self.span = [own, *near, *far], start, 2 * near[0].shape[0]

    def fetch(self, pos_ref, refs, buffer, base, sems, partner):
        steps, half = (len(refs) + 1) // 2, self.span // 2
        owner = lax.bitwise_xor(pos_ref[2], partner)
        step = lax.rem(pos_ref[0] - owner + steps, steps)
        mine = pl.multiple_of(pos_ref[1] * half, half)
        other = pl.multiple_of((1 - pos_ref[1]) * half, half)

        def copies(first, second):
            return [
                pltpu.make_async_copy(
                    source, buffer.at[partner, pl.ds(base + place, half)], sems.at[partner, which]
                )
                for which, (source, place) in enumerate(((first, mine), (second, other)))
            ]

        for distance in range(steps):

            @pl.when(step == distance)
            def _(distance=distance):
                if distance == 0:
                    pair = [refs[0].at[pl.ds(self.start + at, half)] for at in (mine, other)]
                else:
                    pair = [refs[distance], refs[steps - 1 + distance]]
                for copy in copies(*pair):
                    copy.start()

        return copies(refs[1], refs[steps])


def grad_kernel(weights, steps, ranges, pos_ref, cot_ref, *refs):
    held = len(weights.arrays)
    outs, (buffer, sems) = refs[held:-2], refs[-2:]
    order = list(range(1, steps)) + [0]
    copies = {
        partner: weights.fetch(pos_ref, refs[:held], buffer, 0, sems, partner)
        for partner in order
    }
    for partner in order:
        for copy in copies[partner]:
            copy.wait()
        part = lax.dot_general(
            cot_ref[...],
            buffer[partner],
            (((1,), (1,)), ((), ())),
            preferred_element_type=F32,
        )
        if partner == 0:
            outs[0][...] = part.reshape(outs[0].shape)
            continue
        for r, (start, stop) in enumerate(ranges):
            out_ref = outs[1 + r * (steps - 1) + partner - 1]
            rows = outs[0].shape[1]
            for s in range(out_ref.shape[0]):
                out_ref[s] = part[s * rows + start : s * rows + stop].astype(BF16)


def grad_parts(pos, cotangent, weights, steps, ranges):
    seqs, rows, width = cotangent.shape
    span = weights.span
    inside = pl.BlockSpec(memory_space=pltpu.VMEM)
    shapes = [jax.ShapeDtypeStruct((seqs, rows, span), F32)]
    for start, stop in ranges:
        shapes += [jax.ShapeDtypeStruct((seqs, stop - start, span), BF16)] * (steps - 1)
    found = pl.pallas_call(
        functools.partial(grad_kernel, weights, steps, ranges),
        in_specs=[pl.BlockSpec(memory_space=pltpu.SMEM), inside]
        + [pl.BlockSpec(memory_space=pltpu.HBM)] * len(weights.arrays),
        out_specs=[inside] * len(shapes),
        out_shape=shapes,
        scratch_shapes=[
            pltpu.VMEM((steps, span, width), BF16),
            pltpu.SemaphoreType.DMA((steps, 2)),
        ],
        compiler_params=params(24),
        name="grad_parts",
    )(pos, cotangent.reshape(seqs * rows, width), *weights.arrays)
    return found[0], [
        found[1 + r * (steps - 1) : 1 + (r + 1) * (steps - 1)] for r in range(len(ranges))
    ]


def out_kernel(weights, steps, pos_ref, *refs):
    out_ref, buffer, *sems = refs[-2 - len(weights) :]
    copies = {partner: [] for partner in range(steps)}
    for piece, piece_sems in zip(weights, sems):
        held, refs = refs[: len(piece.arrays)], refs[len(piece.arrays) :]
        for partner in range(steps):
            copies[partner] += piece.fetch(
                pos_ref, held, buffer, piece.start, piece_sems, partner
            )
    total = None
    for partner in range(steps):
        for copy in copies[partner]:
            copy.wait()
        left = refs[partner][...].reshape(-1, buffer.shape[1])
        term = jnp.dot(left, buffer[partner], preferred_element_type=F32)
        total = term if total is None else total + term
    out_ref[...] = total.astype(BF16).reshape(out_ref.shape)


def block_output(pos, weights, gated, at, blocks, before):
    steps = len(gated)
    seqs, rows, depth = gated[0].shape
    width = weights[0].arrays[0].shape[1]
    inside = pl.BlockSpec(memory_space=pltpu.VMEM)
    anywhere = pl.BlockSpec(memory_space=pltpu.HBM)
    arrays = [array for piece in weights for array in piece.arrays]
    before = [] if before is None else [before]
    return pl.pallas_call(
        functools.partial(out_kernel, weights, steps),
        grid=(1,),
        in_specs=[pl.BlockSpec(memory_space=pltpu.SMEM)]
        + [anywhere] * len(arrays)
        + [inside] * steps
        + [anywhere] * len(before),
        out_specs=pl.BlockSpec((seqs, rows, width), lambda i: (0, at, 0)),
        out_shape=jax.ShapeDtypeStruct((seqs, blocks * rows, width), BF16),
        scratch_shapes=[pltpu.VMEM((steps, depth, width), BF16)]
        + [pltpu.SemaphoreType.DMA((steps, 2))] * len(weights),
        input_output_aliases={1 + len(arrays) + steps: 0} if before else {},
        compiler_params=params(24),
        name="block_output",
    )(pos, *arrays, *gated, *before)


def mix_grad_kernel(count, start, stop, *refs):
    terms = refs[:count]
    low_ref, high_ref, x_ref, front_ref, w_ref, mix_ref, query_ref = refs[count : count + 7]
    pad = refs[-1]
    seqs, half = x_ref.shape[1], low_ref.shape[1]
    for s in range(seqs):
        query = convolve(x_ref, w_ref, pad, 0, s, front_rows(front_ref, 0, s, half))
        for first, mixed_ref in ((0, low_ref), (half, high_ref)):
            begin, end = max(first, start), min(first + half, stop)
            if begin >= end:
                continue
            at = slice(begin - start, end - start)
            total = terms[0][s, begin:end]
            for term in terms[1:]:
                total = total + term[s, at].astype(F32)
            gated_grad = total.astype(BF16).astype(F32)
            mixed = mixed_ref[s, begin - first : end - first]
            mix_ref[s, at] = (gated_grad * query[begin:end]).astype(BF16)
            query_ref[s, at] = (gated_grad * mixed).astype(BF16)
        if start == 0:
            pack_ref = refs[count + 7]
            pack_ref[s, :HALO] = mix_ref[s, :HALO]
            pack_ref[s, HALO : HALO + EXTRA] = query_ref[s, :EXTRA]
            heads = [x_ref[j, s, :EXTRA].astype(F32)[:8] for j in (1, 2)]
            pack_ref[s, HALO + EXTRA :] = jnp.concatenate(heads, axis=0).astype(BF16)


def mix_grads(own, terms, start, stop, mixed, x, front, short_w, offset):
    seqs, rows, width = own.shape
    half = rows // 2
    first = offset // LANES
    local = lambda count: pl.BlockSpec((seqs, count, LANES), lambda i: (0, 0, i))
    wide = lambda count: pl.BlockSpec((seqs, count, LANES), lambda i: (0, 0, first + i))
    counts = [stop - start] * 2 + [HALO + 2 * EXTRA] * (start == 0)
    return pl.pallas_call(
        functools.partial(mix_grad_kernel, 1 + len(terms), start, stop),
        grid=(width // LANES,),
        in_specs=[local(rows)]
        + [local(stop - start)] * len(terms)
        + [wide(half), wide(half)]
        + [
            pl.BlockSpec((3, seqs, rows, LANES), lambda i: (0, 0, 0, first + i)),
            wide(front.shape[1]),
            pl.BlockSpec((3, 3, LANES), lambda i: (0, 0, first + i)),
        ],
        out_specs=[local(count) for count in counts],
        out_shape=[jax.ShapeDtypeStruct((seqs, count, width), BF16) for count in counts],
        scratch_shapes=[pltpu.VMEM((3 * seqs, rows + 8, LANES), F32)],
        compiler_params=params(),
        name="mix_grads",
    )(own, *terms, *mixed, x, front, short_w)


def join(parts, whole_ref):
    at = 0
    for part_ref in parts:
        whole_ref[:, at : at + part_ref.shape[1]] = part_ref[...]
        at += part_ref.shape[1]


def filter_kernel(group_size, ranges, *refs):
    product_ref, head_ref, front_ref, out_ref, left, columns, mix_ref = refs[ranges:]
    join(refs[:ranges], mix_ref)
    seqs = mix_ref.shape[0]
    rows = out_ref.shape[1]
    groups = LANES // group_size
    lane = lax.broadcasted_iota(jnp.int32, (1, LANES), 1) // group_size
    total = None
    for b in range(mix_ref.shape[1] // rows):
        for s in range(seqs):
            at = slice(s * LANES, (s + 1) * LANES)
            block = mix_ref[s, b * rows : (b + 1) * rows]
            for g in range(groups):
                keep = (lane == g).astype(F32).astype(BF16)
                left[b, g * rows : (g + 1) * rows, at] = block * keep
            if b == 0:
                columns[b, :rows, at] = front_ref[s, :rows]
            else:
                columns[b, :rows, at] = product_ref[s, (b - 1) * rows : b * rows]
            columns[b, rows:, at] = product_ref[s, b * rows : (b + 1) * rows]
            if b < 2:
                start = (1 - b) * rows
                columns[b, start : start + EXTRA, at] = head_ref[s]
        term = lax.dot_general(
            left[b], columns[b], (((1,), (1,)), ((), ())), preferred_element_type=F32
        )
        total = term if total is None else total + term
    span = 2 * rows
    folded = []
    for g in range(groups):
        sum_g = None
        for a in range(rows // 8):
            tile = total[g * rows + a * 8 : g * rows + a * 8 + 8]
            tile = pltpu.roll(tile, (span - a * 8) % span, 1)
            sum_g = tile if sum_g is None else sum_g + tile
        folded.append(sum_g)
    stacked = jnp.stack(folded, axis=0)
    result = None
    for r in range(8):
        row = pltpu.roll(stacked[:, r, :], span - r - 1, 1)
        result = row if result is None else result + row
    out_ref[...] = result[:, :rows]


def filter_sums(mix_grad, product, head, front, block_rows, offset, group_size):
    seqs, rows, _ = product.shape
    width = mix_grad[0].shape[2]
    first = offset // LANES
    groups = LANES // group_size
    blocks = rows // block_rows
    return pl.pallas_call(
        functools.partial(filter_kernel, group_size, len(mix_grad)),
        grid=(width // LANES,),
        in_specs=[
            pl.BlockSpec((seqs, part.shape[1], LANES), lambda i: (0, 0, i)) for part in mix_grad
        ]
        + [
            pl.BlockSpec((seqs, rows, LANES), lambda i: (0, 0, first + i)),
            pl.BlockSpec((seqs, EXTRA, LANES), lambda i: (0, 0, first + i)),
            pl.BlockSpec((seqs, front.shape[1], LANES), lambda i: (0, 0, first + i)),
        ],
        out_specs=pl.BlockSpec((groups, block_rows), lambda i: (i, 0)),
        out_shape=jax.ShapeDtypeStruct((width // group_size, block_rows), F32),
        scratch_shapes=[
            pltpu.VMEM((blocks, groups * block_rows, seqs * LANES), BF16),
            pltpu.VMEM((blocks, 2 * block_rows, seqs * LANES), BF16),
            pltpu.VMEM((seqs, rows, LANES), BF16),
        ],
        compiler_params=params(),
        name="filter_sums",
    )(*mix_grad, product, head, front)


def input_grad_kernel(group_size, ranges, *refs):
    line_ref, back_ref, x_ref, front_ref, w_ref, filter_ref = refs[2 * ranges : 2 * ranges + 6]
    out_ref, sums_ref, band, columns, grads, inputs, edge, mix_ref, query_ref = refs[2 * ranges + 6 :]
    join(refs[:ranges], mix_ref)
    join(refs[ranges : 2 * ranges], query_ref)
    seqs, rows = mix_ref.shape[0], mix_ref.shape[1]
    block = line_ref.shape[1] // 2
    groups = LANES // group_size
    fill_band(line_ref, band, block)
    found = []
    for b in range(rows // block):
        for s in range(seqs):
            at = slice(s * LANES, (s + 1) * LANES)
            columns[b, :block, at] = mix_ref[s, b * block : (b + 1) * block]
            if (b + 1) * block < rows:
                columns[b, block:, at] = mix_ref[s, (b + 1) * block : (b + 2) * block]
            else:
                columns[b, block:, at] = back_ref[s, :block]
        stacked = jnp.dot(band[...], columns[b], preferred_element_type=F32)
        found.append(pick_groups(stacked, block, group_size))
    last = rows // block
    for s in range(seqs):
        at = slice(s * LANES, (s + 1) * LANES)
        columns[last, :HALO, at] = back_ref[s, :HALO]
        columns[last, HALO:, at] = jnp.zeros((2 * block - HALO, LANES), BF16)
    few = jnp.concatenate([band[g * block : g * block + EXTRA] for g in range(groups)], axis=0)
    stacked = jnp.dot(few, columns[last], preferred_element_type=F32)
    beyond = pick_groups(stacked, EXTRA, group_size)
    for s in range(seqs):
        at = slice(s * LANES, (s + 1) * LANES)
        after = []
        for j in (1, 2):
            own = s * 2 + j - 1
            edge[own, 0:8] = x_ref[j, s, rows - 16 :].astype(F32)[8:]
            edge[own, 8:16] = back_ref[s, HALO + EXTRA :].astype(F32)[8 * j - 8 : 8 * j]
            total = w_ref[j, 0:1] * edge[own, 8:16]
            total = total + w_ref[j, 1:2] * edge[own, 7:15]
            total = total + w_ref[j, 2:3] * edge[own, 6:14]
            after.append(total)
        streams = [
            convolve(x_ref, w_ref, inputs, j, s, front_rows(front_ref, j, s, block))
            for j in range(1, 3)
        ]
        inputs[s * 3, 0:8] = front_rows(front_ref, 0, s, block)
        inputs[s * 3, 8 : 8 + rows] = x_ref[0, s].astype(F32)
        for j in range(3):
            own = s * 3 + j
            if j == 0:
                grads[own, :rows] = query_ref[s].astype(F32)
                grads[own, rows:] = back_ref[s, HALO : HALO + EXTRA].astype(F32)[:8]
            else:
                factor = streams[2 - j]
                for b in range(rows // block):
                    part = slice(b * block, (b + 1) * block)
                    value = found[b][:, at] * factor[part]
                    grads[own, part] = value.astype(BF16).astype(F32)
                value = beyond[:8, at] * after[2 - j]
                grads[own, rows:] = value.astype(BF16).astype(F32)
            total = None
            for i in range(3):
                term = w_ref[j, i : i + 1] * grads[own, i : i + rows]
                total = term if total is None else total + term
            out_ref[j, s] = total.astype(BF16)
    for j in range(3):
        for i in range(3):
            total = None
            for s in range(seqs):
                own = s * 3 + j
                term = grads[own, :rows] * inputs[own, 8 - i : 8 - i + rows]
                term = jnp.sum(term, axis=0, keepdims=True)
                total = term if total is None else total + term
            sums_ref[0, groups + j * 3 + i : groups + j * 3 + i + 1] = total
    sums_ref[0, :groups] = filter_ref[...]
    sums_ref[0, groups + 9 :] = jnp.zeros((sums_ref.shape[1] - groups - 9, LANES), F32)


def input_grads(
    line, mix_grad, query_grad, back, x, front, short_w, filter_part, offset, group_size
):
    _, seqs, rows, _ = x.shape
    width = back.shape[2]
    block = line.shape[1] // 2
    first = offset // LANES
    groups = LANES // group_size
    local = lambda count: pl.BlockSpec((seqs, count, LANES), lambda i: (0, 0, i))
    wide3 = lambda *sizes: pl.BlockSpec(sizes + (LANES,), lambda i: (0, 0, first + i))
    wide4 = lambda *sizes: pl.BlockSpec(sizes + (LANES,), lambda i: (0, 0, 0, first + i))
    return pl.pallas_call(
        functools.partial(input_grad_kernel, group_size, len(mix_grad)),
        grid=(width // LANES,),
        in_specs=[local(part.shape[1]) for part in (*mix_grad, *query_grad)]
        + [
            pl.BlockSpec((groups, 2 * block), lambda i: (first + i, 0)),
            local(HALO + 2 * EXTRA),
            wide4(3, seqs, rows),
            wide3(seqs, front.shape[1]),
            wide3(3, 3),
            pl.BlockSpec((groups, block), lambda i: (i, 0)),
        ],
        out_specs=[
            pl.BlockSpec((3, seqs, rows, LANES), lambda i: (0, 0, 0, i)),
            pl.BlockSpec((1, groups + 16, LANES), lambda i: (i, 0, 0)),
        ],
        out_shape=[
            jax.ShapeDtypeStruct((3, seqs, rows, width), BF16),
            jax.ShapeDtypeStruct((width // LANES, groups + 16, LANES), F32),
        ],
        scratch_shapes=[
            pltpu.VMEM((groups * block, 2 * block), BF16),
            pltpu.VMEM((rows // block + 1, 2 * block, seqs * LANES), BF16),
            pltpu.VMEM((3 * seqs, rows + 8, LANES), F32),
            pltpu.VMEM((3 * seqs, rows + 8, LANES), F32),
            pltpu.VMEM((2 * seqs, 16, LANES), F32),
            pltpu.VMEM((seqs, rows, LANES), BF16),
            pltpu.VMEM((seqs, rows, LANES), BF16),
        ],
        compiler_params=params(),
        name="input_grads",
    )(*mix_grad, *query_grad, line, back, x, front, short_w, filter_part)


def total_over(block, axes):
    count = math.prod(lax.axis_size(axis) for axis in axes)
    if count & (count - 1):
        return lax.psum(block, axes)
    step = count // 2
    order = []
    while step:
        order.append(step)
        step //= 2
    for step in order:
        block = block + lax.ppermute(block, axes, [(i, i ^ step) for i in range(count)])
    return block


def shards(projected, short_w, medium_h, out_w, grad_out):
    seqs, rows, _, width = projected.shape
    taps = medium_h.shape[1]
    group_size = width // medium_h.shape[0]
    groups = LANES // group_size
    members = lax.axis_size("grp")
    cores = lax.axis_size("dp")
    length = lax.axis_size("ctx")
    partners = range(members)
    to = lambda block, k: lax.ppermute(block, "grp", [(i, i ^ k) for i in partners])
    around = lambda block: lax.ppermute(block, "ctx", [(i, (i + 1) % length) for i in range(length)])
    swap = lambda block: lax.ppermute(block, "dp", [(0, 1), (1, 0)])
    core = lax.axis_index("dp")
    pos = jnp.stack([lax.axis_index("ctx"), core, lax.axis_index("grp")]).astype(jnp.int32)

    depth = out_w.shape[0]
    ring = depth == width and cores == 2
    cut = width * FIRST // 8 if ring else depth

    def own_half(start, stop):
        half = (stop - start) // cores
        return lax.dynamic_slice_in_dim(out_w, start + core * half, half, axis=0)

    if ring:
        early, near = [around(own_half(0, cut))], [around(own_half(cut, depth))]
    else:
        whole = lax.all_gather(own_half(0, depth), ("ctx", "dp"), axis=0, tiled=True)
        weights = [Gathered(whole, members, 0)]

    x = jnp.transpose(projected, (2, 0, 1, 3))
    filters = medium_h.astype(F32)
    empty = jnp.zeros_like(filters)
    causal = jnp.concatenate([empty[:, :1], filters[:, ::-1], empty[:, 1:]], axis=1)
    anticausal = jnp.concatenate([filters, empty], axis=1)

    product, pack = products(x, short_w, taps)
    mixed_high, gated_high = mix_high(causal, product, x, short_w, taps, group_size)
    high = [gated_high] + [to(gated_high, k) for k in partners[1:]]
    if ring:
        early.append(around(after(early[-1], mixed_high)))
        near.append(around(after(near[-1], mixed_high)))
        for _ in range(length - 3):
            early.append(around(early[-1]))
            near.append(around(after(near[-1], *high[1:])))
        weights = [Passed(out_w, early, [swap(block) for block in early], 0)]

    def send_parts(piece, ranges, ready, before):
        own, parts = grad_parts(pos, after(grad_out, *ready), piece, members, ranges)
        sent = [[after(block, *before) for block in blocks] for blocks in parts]
        return own, [[to(block, k + 1) for k, block in enumerate(blocks)] for blocks in sent]

    ranges = [[(0, rows)]]
    own, got = send_parts(weights[0], ranges[0], high[1:], [])
    owns, gots = [own], [got]
    if ring:
        near[-1] = after(near[-1], got[0][2])
        weights.append(Passed(out_w, near, [swap(block) for block in near], cut))
        ranges.append([(0, rows)])
        own, got = send_parts(weights[1], ranges[1], [], got[0])
        owns.append(own)
        gots.append(got)

    block_out = block_output(pos, weights, high, 1, 2, None)
    front = shift(after(pack, owns[0]), "ctx", 1)
    front = after(front, block_out)
    mixed_low, gated_low, head = mix_low(causal, front, product, x, short_w, taps, group_size)
    sent = after(gated_low, owns[-1])
    low = [gated_low] + [to(sent, k) for k in partners[1:]]

    outs, sums = [], []
    for p, piece in enumerate(weights):
        mix_grad, query_grad, back = [], [], None
        for (start, stop), terms in zip(ranges[p], gots[p]):
            held = after(owns[p], outs[-1], block_out) if p else owns[p]
            found = mix_grads(
                held,
                terms,
                start,
                stop,
                (mixed_low, mixed_high),
                x,
                front,
                short_w,
                piece.start,
            )
            mix_grad.append(found[0])
            query_grad.append(found[1])
            if start == 0:
                back = shift(found[2], "ctx", -1)
        back = after(back, *([] if p else [block_out]))
        folded = filter_sums(mix_grad, product, head, front, taps, piece.start, group_size)
        grad, part = input_grads(
            anticausal,
            mix_grad,
            query_grad,
            back,
            x,
            front,
            short_w,
            folded,
            piece.start,
            group_size,
        )
        outs.append(grad)
        sums.append(part)
    block_out = block_output(pos, weights, low, 0, 2, block_out)
    total = total_over(jnp.concatenate(sums, axis=0), ("dp", "ctx"))

    grad_projected = jnp.transpose(jnp.concatenate(outs, axis=3), (1, 2, 0, 3))
    filter_total = total[:, :groups].reshape(-1, taps)[:, ::-1]
    short_total = jnp.swapaxes(total[:, groups : groups + 9], 0, 1).reshape(3, 3, width)
    seq_total = seqs * cores
    length_total = rows * length
    filter_grad = filter_total / math.sqrt(seq_total * length_total * group_size)
    short_grad = short_total / math.sqrt(seq_total * length_total)
    return (block_out, grad_projected, filter_grad, short_grad)


def solution(mesh):
    in_specs = (
        P("dp", "ctx", None, "grp"),
        P(None, None, "grp"),
        P("grp", None),
        P("ctx", "grp"),
        P("dp", "ctx", "grp"),
    )
    out_specs = (
        P("dp", "ctx", "grp"),
        P("dp", "ctx", None, "grp"),
        P("grp", None),
        P(None, None, "grp"),
    )
    return jax.shard_map(shards, mesh=mesh, in_specs=in_specs, out_specs=out_specs, check_vma=False)
```
